256 devices in a mesh: dp: 16 (over x, y_lo, core), seq: 16 (over y_hi, z).
Axes of the slice: x: 4, y: 4 (y_hi: 2, y_lo: 2; y = y_hi * 2 + y_lo), z: 8, core: 2. Of those that a mesh axis runs over, the one named last changes fastest.
Arguments:
- dna_features: bfloat16 [16, 8192, 768], P('dp', 'seq'), may hold values from -6 to 6
- conv_weight: bfloat16 [5, 768, 1536], P(None, 'dp'), may hold values from -0.09375 to 0.09375
- conv_bias: float32 [1536], replicated, may hold values from -3 to 3
- norm_gain: float32 [1536], replicated, may hold values from 0.1 to 1.9
- query_weight: bfloat16 [1536, 1024], P('dp'), may hold values from -0.15625 to 0.15625
- kv_weight: bfloat16 [1536, 256], P('dp'), may hold values from -0.15625 to 0.15625
- out_weight: bfloat16 [1024, 1536], P('dp'), may hold values from -0.1875 to 0.1875
- head_scale: float32 [8], replicated, may hold values from 1.5 to 64
Outputs:
- tokens: bfloat16 [16, 4096, 1536], P('dp', 'seq')
- encoded: bfloat16 [16, 4096, 1536], P('dp', 'seq')
The draws below stay inside these ranges and needn't reach their ends.
All inputs are finite; a program needn't handle non-finite values.
Results may differ from the reference program's by a relative error of at most 0.0095.
The reference program's roundings to bfloat16 on the way count: a program that leaves them out, or rounds other values in their place, can miss the bound.
Values may be sent and summed in bfloat16 or wider, within the bound.
No kernel may reach another device: no remote copies, remote signals or barrier semaphores. Data moves between devices by JAX's collectives and lax.ppermute only.
A program may use at most 128 MiB of HBM per device.

```python
import math
import jax
import jax.numpy as jnp
from jax import lax

CIN = 768
C = 1536
HEADS = 8
HEAD_SIZE = 128
KW = 5
QW = 1024
BATCH = 16
LENGTH = 4096
POS = 8192


def draw_head_scale(key, part):
    key = jax.random.fold_in(key, 7)
    first = jax.random.fold_in(key, 0)
    base = jnp.exp(jax.random.uniform(first, (HEADS,), jnp.float32, math.log(1.5), math.log(4.0)))
    return base


def levels(key, dims, pieces, least, high):
    loudness = 1.0
    for axis_at, shards_of in pieces:
        draws = jax.random.uniform(jax.random.fold_in(jax.random.fold_in(key, 6), axis_at), (shards_of,), jnp.float32, least / len(pieces), high / len(pieces))
        loudness = loudness * jnp.repeat(jnp.exp(draws), dims[axis_at] // shards_of).reshape((-1,) + (1,) * (len(dims) - 1 - axis_at))
    return loudness


def gaussian(own_key, extent, width, reach, shards=(), held_as=jnp.bfloat16):
    result = width * jax.random.normal(own_key, extent, jnp.float32)
    if shards:
        result = result * levels(own_key, extent, shards, -0.22, 0.18)
    return jnp.clip(result, -reach, reach).astype(held_as)


def setup_inputs(seed: int = 0) -> dict:
    keys = jax.random.split(jax.random.key(seed), 9)
    return {
        "dna_features": gaussian(keys[0], (BATCH, POS, CIN), 1.0, 6.0, ((0, 16), (1, 16))),
        "conv_weight": gaussian(keys[1], (KW, CIN, C), (KW * CIN) ** -0.5, 0.09375, ((1, 16),)),
        "conv_bias": gaussian(keys[2], (C,), 0.5, 3.0, (), jnp.float32),
        "norm_gain": jnp.clip(1.0 + 0.18 * jax.random.normal(keys[3], (C,), jnp.float32), 0.1, 1.9),
        "query_weight": gaussian(keys[4], (C, QW), C ** -0.5, 0.15625, ((0, 16),)),
        "kv_weight": gaussian(keys[5], (C, 2 * HEAD_SIZE), C ** -0.5, 0.15625, ((0, 16),)),
        "out_weight": gaussian(keys[6], (QW, C), QW ** -0.5, 0.1875, ((0, 16),)),
        "head_scale": draw_head_scale(jax.random.fold_in(keys[8], 71), 0),
    }


def conv_sequence(sequence, conv_weight, conv_bias):
    margin = KW // 2
    padded = jnp.pad(sequence, ((margin, margin), (0, 0)))
    running = jnp.zeros((POS, C), jnp.float32)
    for kernel_tap in range(KW):
        running = running + jnp.dot(padded[kernel_tap:kernel_tap + POS], conv_weight[kernel_tap], preferred_element_type=jnp.float32)
    activated = jax.nn.gelu(running + conv_bias)
    return lax.optimization_barrier(jnp.max(activated.reshape(LENGTH, 2, C), axis=1)).astype(jnp.bfloat16)

def attend_block(query_block, keys_all, values_all, head_scale):
    scores = jnp.einsum('qhd,kd->hqk', query_block.astype(jnp.float32), keys_all.astype(jnp.float32))
    scores = scores * (head_scale / math.sqrt(HEAD_SIZE))[:, None, None]
    highest = lax.optimization_barrier(jnp.max(scores, axis=-1, keepdims=True))
    weights = jnp.exp(scores - highest)
    totals = lax.optimization_barrier(jnp.sum(weights, axis=-1))
    rounded = weights.astype(jnp.bfloat16).astype(jnp.float32)
    summed = jnp.einsum('hqk,kd->hqd', rounded, values_all.astype(jnp.float32))
    context = summed / totals[..., None]
    return jnp.transpose(context, (1, 0, 2)).reshape(query_block.shape[0], QW)

def layer_sequence(tokens_seq, norm_gain, query_weight, kv_weight, out_weight, head_scale):
    wide = tokens_seq.astype(jnp.float32)
    stat = lax.optimization_barrier(jnp.mean(jnp.square(wide), axis=-1, keepdims=True))
    normed = (wide * lax.rsqrt(stat + 1e-06) * norm_gain).astype(jnp.bfloat16)
    query_matrix = jnp.dot(normed, query_weight, preferred_element_type=jnp.float32).astype(jnp.bfloat16)
    pairs = jnp.dot(normed, kv_weight, preferred_element_type=jnp.float32).astype(jnp.bfloat16)
    keys_all = pairs[:, :HEAD_SIZE]
    values_all = pairs[:, HEAD_SIZE:]
    block_rows = math.gcd(LENGTH, 512)
    blocks = query_matrix.reshape(LENGTH // block_rows, block_rows, HEADS, HEAD_SIZE)
    context = lax.map(lambda query_block: attend_block(query_block, keys_all, values_all, head_scale), blocks)
    context = context.reshape(LENGTH, QW).astype(jnp.bfloat16)
    update = jnp.dot(context, out_weight, preferred_element_type=jnp.float32)
    return (update + wide).astype(jnp.bfloat16)

def reference(dna_features, conv_weight, conv_bias, norm_gain, query_weight, kv_weight, out_weight, head_scale):
    tokens = lax.map(lambda sequence: conv_sequence(sequence, conv_weight, conv_bias), dna_features)
    encoded = lax.map(lambda tokens_seq: layer_sequence(tokens_seq, norm_gain, query_weight, kv_weight, out_weight, head_scale), tokens)
    return (tokens, encoded)
```

```python
import math

import jax
import jax.numpy as jnp
from jax import lax
from jax.experimental import pallas as pl
from jax.experimental.pallas import tpu as pltpu
from jax.sharding import PartitionSpec as P

CIN = 768
C = 1536
HEADS = 8
HEAD_SIZE = 128
KW = 5
QW = 1024
QUARTER = C // 4
TOKENS = 256
ROWS = CIN // 16
KV = 2 * HEAD_SIZE
REST = KV + QW + QW
BOTH = ("dp", "seq")
LOG2E = math.log2(math.e)
F32 = jnp.float32
BF16 = jnp.bfloat16


def places():
    for dp in range(16):
        for seq in range(16):
            yield dp // 4, dp // 2 % 2, dp % 2, seq // 8, seq % 8


def index(x, y_lo, core, y_hi, z):
    return (x * 4 + y_lo * 2 + core) * 16 + y_hi * 8 + z


def receive(value, source):
    pairs = [(index(*source(*p)), index(*p)) for p in places()]
    return lax.ppermute(value, BOTH, pairs)


def from_core(x, y, c, h, z):
    return x, y, 1 - c, h, z


def from_z_pair(x, y, c, h, z):
    return x, y, c, h, z ^ 1


def from_diagonal(x, y, c, h, z):
    return x, y, 1 - c, h, z ^ 1


def from_x(step):
    return lambda x, y, c, h, z: (x ^ step, y, c, h, z)


def from_y(step):
    def source(x, y, c, h, z):
        at = (h * 2 + y + step) % 4
        return x, at % 2, c, at // 2, z

    return source


def from_y_hi(x, y, c, h, z):
    return x, y, c, 1 - h, z


def from_z(step):
    return lambda x, y, c, h, z: (x, y, c, h, (z + step) % 8)


VMEM = pl.BlockSpec(memory_space=pltpu.VMEM)
SMEM = pl.BlockSpec(memory_space=pltpu.SMEM)
ANY = pl.BlockSpec(memory_space=pl.ANY)


def params(mib):
    return pltpu.CompilerParams(vmem_limit_bytes=mib * 2**20)


def run_copies(copies, sems):
    started = [pltpu.make_async_copy(a, b, sems.at[i]) for i, (a, b) in enumerate(copies)]
    for copy in started:
        copy.start()
    for copy in started:
        copy.wait()


UNITS = tuple(xr * 2 + yr for yr in (0, 1) for xr in (0, 1, 3, 2))


def conv_kernel(at_ref, a_ref, bias_ref, *refs):
    units, outs, (w_ref, sems) = refs[:8], refs[8:12], refs[12:]
    step = pl.program_id(0)

    @pl.when(step == 0)
    def _():
        copies = []
        for rel, unit in zip(UNITS, units):
            row = pl.multiple_of((at_ref[0] ^ rel) * (2 * ROWS), 2 * ROWS)
            copies.append((unit, w_ref.at[:, pl.ds(row, 2 * ROWS), :]))
        run_copies(copies, sems)

    w = w_ref[...].reshape(KW * CIN, QUARTER)
    bias = bias_ref[...]
    even = jnp.dot(a_ref[0, :, : KW * CIN], w, preferred_element_type=F32) + bias
    odd = jnp.dot(a_ref[0, :, CIN:], w, preferred_element_type=F32) + bias
    pooled = jnp.maximum(jax.nn.gelu(even), jax.nn.gelu(odd)).astype(BF16)
    for i, out in enumerate(outs):

        @pl.when(step == i)
        def _(out=out):
            out[...] = pooled


def convolve(chip, blocks, bias, units):
    return pl.pallas_call(
        conv_kernel,
        grid=(4,),
        out_shape=[jax.ShapeDtypeStruct((TOKENS, QUARTER), BF16)] * 4,
        in_specs=[SMEM, pl.BlockSpec((1, TOKENS, 6 * CIN), lambda i: (i, 0, 0)), VMEM] + [ANY] * 8,
        out_specs=[pl.BlockSpec((TOKENS, QUARTER), lambda i: (0, 0))] * 4,
        scratch_shapes=[pltpu.VMEM((KW, CIN, QUARTER), BF16), pltpu.SemaphoreType.DMA((8,))],
        compiler_params=params(40),
        cost_estimate=pl.CostEstimate(flops=6_040_000_000, bytes_accessed=14_000_000, transcendentals=786432),
    )(chip, blocks, bias, *units)


PACKED = tuple(
    (cr * 4 + yr * 2 + pair, slot, xr * 4 + yr * 2 + cr)
    for cr in (0, 1)
    for yr in (0, 1)
    for pair, xs in enumerate(((0, 1), (3, 2)))
    for slot, xr in enumerate(xs)
)


def norm_kernel(at_ref, *refs):
    parts, gain_ref, packed = refs[:4], refs[4], refs[5:13]
    tokens_ref, normed_ref, pairs_ref, w_ref, sems = refs[13:]
    copies = []
    for array, slot, rel in PACKED:
        row = pl.multiple_of((at_ref[0] ^ rel) * 96, 96)
        copies.append((packed[array].at[slot, :, pl.ds(0, KV)], w_ref.at[pl.ds(row, 96), :]))
    for i, part in enumerate(parts):
        column = pl.multiple_of((at_ref[1] ^ i) * QUARTER, QUARTER)
        tokens_ref[:, pl.ds(column, QUARTER)] = part[...]
    wide = tokens_ref[...].astype(F32)
    stat = jnp.mean(jnp.square(wide), axis=-1, keepdims=True)
    normed = (wide * lax.rsqrt(stat + 1e-06) * gain_ref[...]).astype(BF16)
    normed_ref[...] = normed
    run_copies(copies, sems)
    pairs_ref[...] = jnp.dot(normed, w_ref[...], preferred_element_type=F32).astype(BF16)


def norm_and_pairs(at, parts, gain, packed):
    return pl.pallas_call(
        norm_kernel,
        out_shape=[
            jax.ShapeDtypeStruct((TOKENS, C), BF16),
            jax.ShapeDtypeStruct((TOKENS, C), BF16),
            jax.ShapeDtypeStruct((TOKENS, KV), BF16),
        ],
        in_specs=[SMEM] + [VMEM] * 5 + [ANY] * 8,
        out_specs=[VMEM] * 3,
        scratch_shapes=[pltpu.VMEM((C, KV), BF16), pltpu.SemaphoreType.DMA((16,))],
        compiler_params=params(24),
        cost_estimate=pl.CostEstimate(flops=201_000_000, bytes_accessed=3_500_000, transcendentals=0),
    )(at, *parts, gain, *packed)


def query_kernel(at_ref, normed_ref, *refs):
    packed, (out_ref, w_ref, sems) = refs[:8], refs[8:]
    copies = []
    for array, slot, rel in PACKED:
        row = pl.multiple_of((at_ref[0] ^ rel) * 96, 96)
        copies.append((packed[array].at[slot, :, pl.ds(KV, QW)], w_ref.at[pl.ds(row, 96), :]))
    run_copies(copies, sems)
    queries = jnp.dot(normed_ref[...], w_ref[...], preferred_element_type=F32).astype(BF16)
    for head in range(HEADS):
        out_ref[head] = queries[:, head * HEAD_SIZE : (head + 1) * HEAD_SIZE]


def project_queries(at, normed, packed):
    return pl.pallas_call(
        query_kernel,
        out_shape=jax.ShapeDtypeStruct((HEADS, TOKENS, HEAD_SIZE), BF16),
        in_specs=[SMEM, VMEM] + [ANY] * 8,
        out_specs=VMEM,
        scratch_shapes=[pltpu.VMEM((C, QW), BF16), pltpu.SemaphoreType.DMA((16,))],
        compiler_params=params(24),
        cost_estimate=pl.CostEstimate(flops=805_000_000, bytes_accessed=4_500_000, transcendentals=0),
    )(at, normed, *packed)


def attend_kernel(n_blocks, first, scale_ref, q_ref, *refs):
    kvs, refs = refs[:n_blocks], refs[n_blocks:]
    if first:
        top_out, total_out, sum_out = refs
    else:
        top_ref, total_ref, sum_ref, top_out, total_out, sum_out = refs
    scale = scale_ref[pl.program_id(0)]
    q = q_ref[0]
    lanes = (TOKENS, HEAD_SIZE)
    scores, values = [], []
    for kv in kvs:
        keys = kv[:, :HEAD_SIZE]
        scores.append(
            lax.dot_general(q, keys, (((1,), (1,)), ((), ())), preferred_element_type=F32)
        )
        values.append(kv[:, HEAD_SIZE:])
    width = scores[0].shape[1]
    tall = scores[0]
    for s in scores[1:]:
        tall = jnp.maximum(tall, s)
    best = tall[:, :HEAD_SIZE]
    for i in range(1, width // HEAD_SIZE):
        best = jnp.maximum(best, tall[:, i * HEAD_SIZE : (i + 1) * HEAD_SIZE])
    top = jnp.broadcast_to(jnp.max(best, axis=1, keepdims=True), lanes)
    if not first:
        old = top_ref[0]
        top = jnp.maximum(top, old)
        fade = jnp.exp2((old - top) * scale)
    total = jnp.zeros(lanes, F32)
    summed = jnp.zeros(lanes, F32)
    for s, v in zip(scores, values):
        pieces = []
        for i in range(width // HEAD_SIZE):
            e = jnp.exp2((s[:, i * HEAD_SIZE : (i + 1) * HEAD_SIZE] - top) * scale)
            total = total + e
            pieces.append(e.astype(BF16))
        weights = jnp.concatenate(pieces, axis=1)
        summed = summed + jnp.dot(weights, v, preferred_element_type=F32)
    if not first:
        total = total + total_ref[0] * fade
        summed = summed + sum_ref[0] * fade
    top_out[0] = top
    total_out[0] = total
    sum_out[0] = summed


def attend(scale, queries, kvs, state):
    head = pl.BlockSpec((1, TOKENS, HEAD_SIZE), lambda h: (h, 0, 0))
    keys = sum(kv.shape[0] for kv in kvs)
    return pl.pallas_call(
        lambda *refs: attend_kernel(len(kvs), state is None, *refs),
        grid=(HEADS,),
        out_shape=[jax.ShapeDtypeStruct((HEADS, TOKENS, HEAD_SIZE), F32)] * 3,
        in_specs=[SMEM, head]
        + [pl.BlockSpec(kv.shape, lambda h: (0, 0)) for kv in kvs]
        + ([] if state is None else [head] * 3),
        out_specs=[head] * 3,
        compiler_params=params(32),
        cost_estimate=pl.CostEstimate(
            flops=4 * QW * TOKENS * keys,
            bytes_accessed=6_000_000,
            transcendentals=HEADS * TOKENS * keys,
        ),
    )(scale, queries, *kvs, *(state or ()))


def out_kernel(at_ref, total_ref, sum_ref, tokens_ref, *refs):
    packed, (out_ref, w_ref, sems) = refs[:8], refs[8:]
    copies = []
    for array, slot, rel in PACKED:
        row = pl.multiple_of((at_ref[0] ^ rel) * 64, 64)
        late = pl.multiple_of((at_ref[0] ^ rel) * 64 + 32, 32)
        source, start = packed[array], KV + QW
        copies.append((source.at[slot, pl.ds(0, 64), pl.ds(start, 1024)], w_ref.at[pl.ds(row, 64), pl.ds(0, 1024)]))
        copies.append((source.at[slot, pl.ds(64, 32), pl.ds(start, 512)], w_ref.at[pl.ds(row, 32), pl.ds(1024, 512)]))
        copies.append((source.at[slot, pl.ds(64, 32), pl.ds(start + 512, 512)], w_ref.at[pl.ds(late, 32), pl.ds(1024, 512)]))
    run_copies(copies, sems)
    heads = []
    for head in range(HEADS):
        total = jnp.sum(total_ref[head], axis=1, keepdims=True)
        heads.append((sum_ref[head] / total).astype(BF16))
    context = jnp.concatenate(heads, axis=1)
    update = jnp.dot(context, w_ref[...], preferred_element_type=F32)
    out_ref[...] = (update + tokens_ref[...].astype(F32)).astype(BF16)


def project_out(at, total, summed, tokens, packed):
    return pl.pallas_call(
        out_kernel,
        out_shape=jax.ShapeDtypeStruct((TOKENS, C), BF16),
        in_specs=[SMEM] + [VMEM] * 3 + [ANY] * 8,
        out_specs=VMEM,
        scratch_shapes=[pltpu.VMEM((QW, C), BF16), pltpu.SemaphoreType.DMA((48,))],
        compiler_params=params(32),
        cost_estimate=pl.CostEstimate(flops=805_000_000, bytes_accessed=7_000_000, transcendentals=0),
    )(at, total, summed, tokens, *packed)


def after(value, first):
    return lax.optimization_barrier((value, first))


def on_device(
    dna_features, conv_weight, conv_bias, norm_gain, query_weight, kv_weight, out_weight, head_scale
):
    dp, seq = lax.axis_index("dp"), lax.axis_index("seq")
    core, z = dp % 2, seq % 8
    quarter = z % 2 * 2 + core
    at = jnp.stack([dp, quarter]).astype(jnp.int32)

    shape = (KW, ROWS, QUARTER)
    keep = lax.dynamic_slice(conv_weight, (0, 0, quarter * QUARTER), shape)
    give = lax.dynamic_slice(conv_weight, (0, 0, (quarter ^ 1) * QUARTER), shape)
    got = receive(give, from_core)
    unit = jnp.concatenate(
        [jnp.where(core == 0, keep, got), jnp.where(core == 0, got, keep)], axis=1
    )
    x1, x3 = receive(unit, from_x(1)), receive(unit, from_x(3))
    y0 = receive(unit, from_y(1))
    x2 = receive(unit, from_x(2))
    y1, y3 = receive(x1, from_y(-1)), receive(x3, from_y(1))
    y2 = receive(x2, from_y(-1))
    units = (unit, x1, x3, x2, y0, y1, y3, y2)

    rows = dna_features.reshape(TOKENS, 2 * CIN)
    up = [(i, i + 1) for i in range(15)]
    before = lax.ppermute(rows[-1:], "seq", up)
    behind = lax.ppermute(rows[:1], "seq", [(j, i) for i, j in up])
    rows = jnp.concatenate([before, rows, behind], axis=0)
    rows_z = receive(rows, from_z_pair)
    rows_c = receive(rows, from_core)
    rows_d = receive(rows_z, from_core)
    blocks = jnp.stack(
        [
            jnp.concatenate([r[:TOKENS], r[1 : TOKENS + 1], r[2:]], axis=1)
            for r in (rows_d, rows_z, rows_c, rows)
        ]
    )
    bias = lax.dynamic_slice(conv_bias.reshape(1, C), (0, quarter * QUARTER), (1, QUARTER))

    tail = out_weight[:, QW:]
    packed_out = jnp.concatenate(
        [out_weight[:, :QW], jnp.concatenate([tail[:32], tail[32:]], axis=1)], axis=0
    )
    packed = jnp.concatenate([kv_weight, query_weight, packed_out], axis=1)
    packed, x2 = after(packed, x2)
    px1, px3, px2 = (receive(packed, from_x(s)) for s in (1, 3, 2))
    near = [jnp.stack([packed, px1]), jnp.stack([px3, px2])]
    near = near + [receive(near[0], from_y(1)), receive(near[1], from_y(-1))]
    packed = near + [receive(g, from_core) for g in near]

    t_d, t_z, t_c, t_own = convolve(at[:1] // 2, blocks, bias, units)
    parts = (t_own, receive(t_c, from_core), receive(t_z, from_z_pair), receive(t_d, from_diagonal))
    tokens, normed, pairs = norm_and_pairs(at, parts, norm_gain.reshape(1, C), packed)

    both = jnp.concatenate([pairs, receive(pairs, from_y_hi)], axis=0)
    below, above = receive(both, from_z(-1)), receive(both, from_z(1))
    groups = [[both], [below, above]]
    for _ in range(2):
        below, above = receive(below, from_z(-1)), receive(above, from_z(1))
        groups.append([below, above])
    groups.append([receive(below[:TOKENS], from_z(-1)), receive(above[TOKENS:], from_z(1))])

    queries = project_queries(at, normed, packed)
    scale = head_scale * (LOG2E / math.sqrt(HEAD_SIZE))
    state = None
    for group in groups:
        state = attend(scale, queries, group, state)
    encoded = project_out(at, state[1], state[2], tokens, packed)
    return tokens[None], encoded[None]


def solution(mesh):
    in_specs = (
        P("dp", "seq", None),
        P(None, "dp", None),
        P(),
        P(),
        P("dp", None),
        P("dp", None),
        P("dp", None),
        P(),
    )
    out_specs = (P("dp", "seq", None), P("dp", "seq", None))
    return jax.shard_map(
        on_device, mesh=mesh, in_specs=in_specs, out_specs=out_specs, check_vma=False
    )
```

```python
import functools
import math

import jax
import jax.numpy as jnp
from jax import lax
from jax.experimental import pallas as pl
from jax.experimental.pallas import tpu as pltpu
from jax.sharding import PartitionSpec as P

CIN = 768
C = 1536
HEADS = 8
HEAD_SIZE = 128
KW = 5
QW = 1024
QUARTER = C // 4
TOKENS = 256
ROWS = CIN // 16
KV = 2 * HEAD_SIZE
BOTH = ("dp", "seq")
LOG2E = math.log2(math.e)
F32 = jnp.float32
BF16 = jnp.bfloat16


def places():
    for dp in range(16):
        for seq in range(16):
            yield dp // 4, dp // 2 % 2, dp % 2, seq // 8, seq % 8


def index(x, y_lo, core, y_hi, z):
    return (x * 4 + y_lo * 2 + core) * 16 + y_hi * 8 + z


def receive(value, source):
    pairs = [(index(*source(*p)), index(*p)) for p in places()]
    return lax.ppermute(value, BOTH, pairs)


def from_core(x, y, c, h, z):
    return x, y, 1 - c, h, z


def from_z_pair(x, y, c, h, z):
    return x, y, c, h, z ^ 1


def from_diagonal(x, y, c, h, z):
    return x, y, 1 - c, h, z ^ 1


def from_x(step):
    return lambda x, y, c, h, z: (x ^ step, y, c, h, z)


def from_y(step):
    def source(x, y, c, h, z):
        at = (h * 2 + y + step) % 4
        return x, at % 2, c, at // 2, z

    return source


def from_y_hi(x, y, c, h, z):
    return x, y, c, 1 - h, z


def from_z(step):
    return lambda x, y, c, h, z: (x, y, c, h, (z + step) % 8)


VMEM = pl.BlockSpec(memory_space=pltpu.VMEM)
SMEM = pl.BlockSpec(memory_space=pltpu.SMEM)
ANY = pl.BlockSpec(memory_space=pl.ANY)


def params(mib):
    return pltpu.CompilerParams(vmem_limit_bytes=mib * 2**20)


def run_copies(copies, sems):
    started = [pltpu.make_async_copy(a, b, sems.at[i]) for i, (a, b) in enumerate(copies)]
    for copy in started:
        copy.start()
    for copy in started:
        copy.wait()


UNITS = ((0, None), (2, None), (6, None), (4, 0), (4, 1), (1, None), (3, None), (7, None), (5, 0), (5, 1))


def conv_kernel(at_ref, a_ref, bias_ref, *refs):
    units, outs, (w_ref, sems) = refs[:10], refs[10:12], refs[12:]
    step = pl.program_id(0)

    @pl.when(step == 0)
    def _():
        copies = []
        for (rel, core), unit in zip(UNITS, units):
            rows = 2 * ROWS if core is None else ROWS
            row = pl.multiple_of((at_ref[0] ^ rel) * (2 * ROWS) + (core or 0) * ROWS, ROWS)
            copies.append((unit, w_ref.at[:, pl.ds(row, rows), :]))
        run_copies(copies, sems)

    w = w_ref[...].reshape(KW * CIN, QUARTER)
    bias = bias_ref[...]
    even = jnp.dot(a_ref[0, :, : KW * CIN], w, preferred_element_type=F32) + bias
    odd = jnp.dot(a_ref[0, :, CIN:], w, preferred_element_type=F32) + bias
    pooled = jnp.maximum(jax.nn.gelu(even), jax.nn.gelu(odd)).astype(BF16)
    for i, out in enumerate(outs):

        @pl.when(step == i)
        def _(out=out):
            out[...] = pooled


def convolve(chip, blocks, bias, units):
    return pl.pallas_call(
        conv_kernel,
        grid=(2,),
        out_shape=[jax.ShapeDtypeStruct((TOKENS, QUARTER), BF16)] * 2,
        in_specs=[SMEM, pl.BlockSpec((1, TOKENS, 6 * CIN), lambda i: (i, 0, 0)), VMEM] + [ANY] * 10,
        out_specs=[pl.BlockSpec((TOKENS, QUARTER), lambda i: (0, 0))] * 2,
        scratch_shapes=[pltpu.VMEM((KW, CIN, QUARTER), BF16), pltpu.SemaphoreType.DMA((10,))],
        compiler_params=params(24),
        cost_estimate=pl.CostEstimate(flops=6_000_000_000, bytes_accessed=8_000_000, transcendentals=393216),
    )(chip, blocks, bias, *units)


def norm_kernel(at_ref, *refs):
    parts, gain_ref, w_ref = refs[:4], refs[4], refs[5]
    tokens_ref, normed_ref, pairs_ref = refs[6:]
    for i, part in enumerate(parts):
        column = pl.multiple_of((at_ref[1] ^ i) * QUARTER, QUARTER)
        tokens_ref[:, pl.ds(column, QUARTER)] = part[...]
    wide = tokens_ref[...].astype(F32)
    stat = jnp.mean(jnp.square(wide), axis=-1, keepdims=True)
    normed = (wide * lax.rsqrt(stat + 1e-06) * gain_ref[...]).astype(BF16)
    normed_ref[...] = normed
    pairs_ref[...] = jnp.dot(normed, w_ref[...], preferred_element_type=F32).astype(BF16)


def norm_and_pairs(at, parts, gain, weights):
    return pl.pallas_call(
        norm_kernel,
        grid=(1,),
        out_shape=[
            jax.ShapeDtypeStruct((TOKENS, C), BF16),
            jax.ShapeDtypeStruct((TOKENS, C), BF16),
            jax.ShapeDtypeStruct((TOKENS, KV), BF16),
        ],
        in_specs=[SMEM] + [VMEM] * 5 + [pl.BlockSpec((C, KV), lambda i: (0, QW // KV))],
        out_specs=[VMEM] * 3,
        compiler_params=params(20),
        cost_estimate=pl.CostEstimate(flops=2_000_000_000, bytes_accessed=3_500_000, transcendentals=0),
    )(at, *parts, gain, weights)


def query_kernel(normed_ref, w_ref, out_ref):
    queries = jnp.dot(normed_ref[...], w_ref[...], preferred_element_type=F32).astype(BF16)
    for head in range(HEADS):
        out_ref[head] = queries[:, head * HEAD_SIZE : (head + 1) * HEAD_SIZE]


def project_queries(normed, weights):
    return pl.pallas_call(
        query_kernel,
        grid=(1,),
        out_shape=jax.ShapeDtypeStruct((HEADS, TOKENS, HEAD_SIZE), BF16),
        in_specs=[VMEM, pl.BlockSpec((C, QW), lambda i: (0, 0))],
        out_specs=VMEM,
        compiler_params=params(20),
        cost_estimate=pl.CostEstimate(flops=2_000_000_000, bytes_accessed=4_500_000, transcendentals=0),
    )(normed, weights)


def attend_head(head, first, scale_ref, q_ref, kvs, old_refs, new_refs):
    scale = scale_ref[head]
    q = q_ref[head]
    lanes = (TOKENS, HEAD_SIZE)
    scores = [
        lax.dot_general(
            q, kv[:, :HEAD_SIZE], (((1,), (1,)), ((), ())), preferred_element_type=F32
        )
        for kv in kvs
    ]
    pieces = [
        [s[:, i : i + HEAD_SIZE] for i in range(0, s.shape[1], HEAD_SIZE)] for s in scores
    ]
    best = functools.reduce(jnp.maximum, [piece for group in pieces for piece in group])
    top = jnp.broadcast_to(jnp.max(best, axis=1, keepdims=True), lanes)
    if not first:
        old = old_refs[0][head]
        top = jnp.maximum(top, old)
        fade = jnp.exp2((old - top) * scale)
    total = jnp.zeros(lanes, F32)
    summed = jnp.zeros(lanes, F32)
    for group, kv in zip(pieces, kvs):
        weights = []
        for piece in group:
            e = jnp.exp2((piece - top) * scale)
            total = total + e
            weights.append(e.astype(BF16))
        summed = summed + jnp.dot(
            jnp.concatenate(weights, axis=1), kv[:, HEAD_SIZE:], preferred_element_type=F32
        )
    if not first:
        total = total + old_refs[1][head] * fade
        summed = summed + old_refs[2][head] * fade
    new_refs[0][head] = top
    new_refs[1][head] = total
    new_refs[2][head] = summed


def attend_kernel(n_blocks, first, scale_ref, q_ref, *refs):
    kvs, states = refs[:n_blocks], refs[n_blocks:]

    @pl.loop(0, HEADS, step=2)
    def _(head):
        for i in range(2):
            attend_head(head + i, first, scale_ref, q_ref, kvs, states[:3], states[-3:])


def attend(scale, queries, kvs, state):
    keys = sum(kv.shape[0] for kv in kvs)
    state = state or ()
    return pl.pallas_call(
        lambda *refs: attend_kernel(len(kvs), not state, *refs),
        out_shape=[jax.ShapeDtypeStruct((HEADS, TOKENS, HEAD_SIZE), F32)] * 3,
        in_specs=[SMEM] + [VMEM] * (1 + len(kvs) + len(state)),
        out_specs=[VMEM] * 3,
        compiler_params=params(20),
        cost_estimate=pl.CostEstimate(
            flops=24 * QW * TOKENS * keys,
            bytes_accessed=6_000_000,
            transcendentals=HEADS * TOKENS * keys,
        ),
    )(scale, queries, *kvs, *state)


def out_kernel(total_ref, sum_ref, tokens_ref, w_ref, out_ref):
    heads = []
    for head in range(HEADS):
        total = jnp.sum(total_ref[head], axis=1, keepdims=True)
        heads.append((sum_ref[head] / total).astype(BF16))
    context = jnp.concatenate(heads, axis=1)
    update = jnp.dot(context, w_ref[...], preferred_element_type=F32)
    out_ref[...] = (update + tokens_ref[...].astype(F32)).astype(BF16)


def project_out(total, summed, tokens, weights):
    return pl.pallas_call(
        out_kernel,
        out_shape=jax.ShapeDtypeStruct((TOKENS, C), BF16),
        in_specs=[VMEM] * 4,
        out_specs=VMEM,
        compiler_params=params(24),
        cost_estimate=pl.CostEstimate(flops=2_000_000_000, bytes_accessed=7_000_000, transcendentals=0),
    )(total, summed, tokens, weights)


def on_device(
    dna_features, conv_weight, conv_bias, norm_gain, query_weight, kv_weight, out_weight, head_scale
):
    dp, seq = lax.axis_index("dp"), lax.axis_index("seq")
    core, z = dp % 2, seq % 8
    quarter = z % 2 * 2 + core
    at = jnp.stack([dp, quarter]).astype(jnp.int32)

    shape = (KW, ROWS, QUARTER)
    keep = lax.dynamic_slice(conv_weight, (0, 0, quarter * QUARTER), shape)
    give = lax.dynamic_slice(conv_weight, (0, 0, (quarter ^ 1) * QUARTER), shape)
    got = receive(give, from_core)
    unit = jnp.concatenate(
        [jnp.where(core == 0, keep, got), jnp.where(core == 0, got, keep)], axis=1
    )
    x1, x3 = receive(unit, from_x(1)), receive(unit, from_x(3))
    y0 = receive(unit, from_y(1))
    x2a, x2b = receive(x3[:, :ROWS], from_x(1)), receive(x1[:, ROWS:], from_x(3))
    y1, y3 = receive(x1, from_y(-1)), receive(x3, from_y(1))
    y2a, y2b = receive(x2a, from_y(-1)), receive(x2b, from_y(1))
    units = (unit, x1, x3, x2a, x2b, y0, y1, y3, y2a, y2b)

    rows = dna_features.reshape(TOKENS, 2 * CIN)
    up = [(i, i + 1) for i in range(15)]
    before = lax.ppermute(rows[-1:], "seq", up)
    behind = lax.ppermute(rows[:1], "seq", [(j, i) for i, j in up])
    rows = jnp.concatenate([before, rows, behind], axis=0)
    rows_z = receive(rows, from_z_pair)
    rows_c = receive(rows, from_core)
    rows_d = receive(rows_z, from_core)
    far, near = (
        jnp.stack([jnp.concatenate([r[:TOKENS], r[1 : TOKENS + 1], r[2:]], axis=1) for r in pair])
        for pair in ((rows_d, rows_z), (rows_c, rows))
    )
    bias = lax.dynamic_slice(conv_bias.reshape(1, C), (0, quarter * QUARTER), (1, QUARTER))

    projections = jnp.concatenate([query_weight, kv_weight], axis=1)
    projections = lax.all_gather(projections, "dp", axis=0, tiled=True)
    out_weights = lax.all_gather(out_weight, "dp", axis=0, tiled=True)

    t_d, t_z = convolve(at[:1] // 2, far, bias, units)
    t_c, t_own = convolve(at[:1] // 2, near, bias, units)
    parts = (t_own, receive(t_c, from_core), receive(t_z, from_z_pair), receive(t_d, from_diagonal))
    tokens, normed, pairs = norm_and_pairs(at, parts, norm_gain.reshape(1, C), projections)

    queries = project_queries(normed, projections)
    scale = head_scale * (LOG2E / math.sqrt(HEAD_SIZE))

    both = jnp.concatenate([pairs, receive(pairs, from_y_hi)], axis=0)
    below, above = receive(both, from_z(-1)), receive(both, from_z(1))
    state = attend(scale, queries, [both], None)
    for step in range(3):
        if step < 2:
            coming = receive(below, from_z(-1)), receive(above, from_z(1))
        else:
            coming = receive(below[:TOKENS], from_z(-1)), receive(above[TOKENS:], from_z(1))
        state = attend(scale, queries, [below, above], state)
        below, above = coming
    state = attend(scale, queries, [below, above], state)
    encoded = project_out(state[1], state[2], tokens, out_weights)
    return tokens[None], encoded[None]


def solution(mesh):
    in_specs = (
        P("dp", "seq", None),
        P(None, "dp", None),
        P(),
        P(),
        P("dp", None),
        P("dp", None),
        P("dp", None),
        P(),
    )
    out_specs = (P("dp", "seq", None), P("dp", "seq", None))
    return jax.shard_map(
        on_device, mesh=mesh, in_specs=in_specs, out_specs=out_specs, check_vma=False
    )
```

```python
import functools
import math

import jax
import jax.numpy as jnp
from jax import lax
from jax.experimental import pallas as pl
from jax.experimental.pallas import tpu as pltpu
from jax.sharding import PartitionSpec as P

CIN = 768
C = 1536
HEADS = 8
HEAD_SIZE = 128
KW = 5
QW = 1024
QUARTER = C // 4
TOKENS = 256
ROWS = CIN // 16
KV = 2 * HEAD_SIZE
BOTH = ("dp", "seq")
LOG2E = math.log2(math.e)
F32 = jnp.float32
BF16 = jnp.bfloat16


def places():
    for dp in range(16):
        for seq in range(16):
            yield dp // 4, dp // 2 % 2, dp % 2, seq // 8, seq % 8


def index(x, y_lo, core, y_hi, z):
    return (x * 4 + y_lo * 2 + core) * 16 + y_hi * 8 + z


def receive(value, source):
    pairs = [(index(*source(*p)), index(*p)) for p in places()]
    return lax.ppermute(value, BOTH, pairs)


def from_core(x, y, c, h, z):
    return x, y, 1 - c, h, z


def from_z_pair(x, y, c, h, z):
    return x, y, c, h, z ^ 1


def from_diagonal(x, y, c, h, z):
    return x, y, 1 - c, h, z ^ 1


def from_x(step):
    return lambda x, y, c, h, z: (x ^ step, y, c, h, z)


def from_y(step):
    def source(x, y, c, h, z):
        at = (h * 2 + y + step) % 4
        return x, at % 2, c, at // 2, z

    return source


def from_y_hi(x, y, c, h, z):
    return x, y, c, 1 - h, z


def from_z(step):
    return lambda x, y, c, h, z: (x, y, c, h, (z + step) % 8)


VMEM = pl.BlockSpec(memory_space=pltpu.VMEM)
SMEM = pl.BlockSpec(memory_space=pltpu.SMEM)
ANY = pl.BlockSpec(memory_space=pl.ANY)


def params(mib):
    return pltpu.CompilerParams(vmem_limit_bytes=mib * 2**20)


def start_copies(copies, sems):
    started = [pltpu.make_async_copy(a, b, sems.at[i]) for i, (a, b) in enumerate(copies)]
    for copy in started:
        copy.start()
    return started


def wait_copies(started):
    for copy in started:
        copy.wait()


def pack_kernel(n_weights, *refs):
    weights, packed_ref, start = refs[:n_weights], refs[-1], 0
    for weight in weights:
        packed_ref[:, start : start + weight.shape[1]] = weight[...]
        start += weight.shape[1]


def pack(weights, done):
    rows, columns = weights[0].shape[0], sum(w.shape[1] for w in weights)
    return pl.pallas_call(
        functools.partial(pack_kernel, len(weights)),
        out_shape=jax.ShapeDtypeStruct((rows, columns), BF16),
        in_specs=[VMEM] * len(weights) + [ANY] * len(done),
        out_specs=VMEM,
        compiler_params=params(8),
    )(*weights, *done)


def pack_weights_kernel(query_ref, kv_ref, out_ref, done_ref, packed_ref):
    packed_ref[:, :QW] = query_ref[...]
    packed_ref[:, QW : QW + KV] = kv_ref[...]
    packed_ref[: QW // 16, QW + KV :] = out_ref[:, :QW]
    packed_ref[QW // 16 :, QW + KV : QW + KV + 512] = out_ref[:32, QW:]
    packed_ref[QW // 16 :, QW + KV + 512 :] = out_ref[32:, QW:]


def pack_weights(query_weight, kv_weight, out_weight, done):
    return pl.pallas_call(
        pack_weights_kernel,
        out_shape=jax.ShapeDtypeStruct((C // 16, QW + KV + QW), BF16),
        in_specs=[VMEM] * 3 + [ANY],
        out_specs=VMEM,
        compiler_params=params(8),
    )(query_weight, kv_weight, out_weight, done)


CHIPS = (0, 2, 6, 4, 1, 3, 7, 5)


def from_chips(weight):
    low = jnp.concatenate([weight, receive(weight, from_x(1))], axis=0)
    high = jnp.concatenate([receive(weight, from_x(step)) for step in (3, 2)], axis=0)
    return [low, high, receive(low, from_y(1)), receive(high, from_y(-1))]


def stack_kernel(*refs):
    arrays, (first_ref, second_ref, sems) = refs[:4], refs[-3:]
    rows, columns = arrays[0].shape[0], first_ref.shape[1]
    copies = []
    for i, array in enumerate(arrays):
        for out_ref, start in ((first_ref, 0), (second_ref, columns)):
            part = array.at[:, pl.ds(start, out_ref.shape[1])]
            copies.append((part, out_ref.at[pl.ds(i * rows, rows), :]))
    wait_copies(start_copies(copies, sems))


def stack(arrays, done):
    rows = arrays[0].shape[0] * 4
    return pl.pallas_call(
        stack_kernel,
        out_shape=[jax.ShapeDtypeStruct((rows, columns), BF16) for columns in (QW + KV, QW)],
        in_specs=[ANY] * (4 + len(done)),
        out_specs=[VMEM] * 2,
        scratch_shapes=[pltpu.SemaphoreType.DMA((8,))],
        compiler_params=params(8),
    )(*arrays, *done)


def place(at_ref, arrays, columns, w_ref, sems):
    rows, copies = C // 16, []
    for core, array in enumerate(arrays):
        for slot, rel in enumerate(CHIPS):
            row = pl.multiple_of((at_ref[0] ^ (rel * 2 + core)) * rows, rows)
            copies.append((array.at[pl.ds(slot * rows, rows), columns], w_ref.at[pl.ds(row, rows), :]))
    return start_copies(copies, sems)


def place_out(at_ref, arrays, w_ref, sems):
    copies = []
    for core, array in enumerate(arrays):
        for slot, rel in enumerate(CHIPS):
            row = pl.multiple_of((at_ref[0] ^ (rel * 2 + core)) * 64, 64)
            late = pl.multiple_of(row + 32, 32)
            at, start = slot * 96, 0
            whole = array.at[pl.ds(at, 64), pl.ds(start, QW)]
            copies.append((whole, w_ref.at[pl.ds(row, 64), pl.ds(0, QW)]))
            for half, to in enumerate((row, late)):
                tail = array.at[pl.ds(at + 64, 32), pl.ds(start + half * 512, 512)]
                copies.append((tail, w_ref.at[pl.ds(to, 32), pl.ds(QW, 512)]))
    return start_copies(copies, sems)


def conv_kernel(at_ref, a_ref, bias_ref, *refs):
    units, outs, (w_ref, sems) = refs[:4], refs[4:6], refs[6:]
    step = pl.program_id(0)

    @pl.when(step == 0)
    def _():
        copies = []
        for i, rel in enumerate(CHIPS):
            row = pl.multiple_of((at_ref[0] ^ rel) * (2 * ROWS), 2 * ROWS)
            unit = units[i // 2].at[:, pl.ds(i % 2 * 2 * ROWS, 2 * ROWS), :]
            copies.append((unit, w_ref.at[:, pl.ds(row, 2 * ROWS), :]))
        wait_copies(start_copies(copies, sems))

    w = w_ref[...].reshape(KW * CIN, QUARTER)
    bias = bias_ref[...]
    even = jnp.dot(a_ref[0, :, : KW * CIN], w, preferred_element_type=F32) + bias
    odd = jnp.dot(a_ref[0, :, CIN:], w, preferred_element_type=F32) + bias
    pooled = jnp.maximum(jax.nn.gelu(even), jax.nn.gelu(odd)).astype(BF16)
    for i, out in enumerate(outs):

        @pl.when(step == i)
        def _(out=out):
            out[...] = pooled


def convolve(chip, blocks, bias, units):
    return pl.pallas_call(
        conv_kernel,
        grid=(2,),
        out_shape=[jax.ShapeDtypeStruct((TOKENS, QUARTER), BF16)] * 2,
        in_specs=[SMEM, pl.BlockSpec((1, TOKENS, 6 * CIN), lambda i: (i, 0, 0)), VMEM] + [ANY] * 4,
        out_specs=[pl.BlockSpec((TOKENS, QUARTER), lambda i: (0, 0))] * 2,
        scratch_shapes=[pltpu.VMEM((KW, CIN, QUARTER), BF16), pltpu.SemaphoreType.DMA((8,))],
        compiler_params=params(24),
        cost_estimate=pl.CostEstimate(flops=6_000_000_000, bytes_accessed=8_000_000, transcendentals=393216),
    )(chip, blocks, bias, *units)


def norm_kernel(at_ref, *refs):
    parts, gain_ref, arrays = refs[:4], refs[4], refs[5:7]
    tokens_ref, normed_ref, pairs_ref, w_ref, sems = refs[7:]
    copies = place(at_ref, arrays, pl.ds(QW, KV), w_ref, sems)
    for i, part in enumerate(parts):
        column = pl.multiple_of((at_ref[1] ^ i) * QUARTER, QUARTER)
        tokens_ref[:, pl.ds(column, QUARTER)] = part[...]
    wide = tokens_ref[...].astype(F32)
    stat = jnp.mean(jnp.square(wide), axis=-1, keepdims=True)
    normed = (wide * lax.rsqrt(stat + 1e-06) * gain_ref[...]).astype(BF16)
    normed_ref[...] = normed
    wait_copies(copies)
    pairs_ref[...] = jnp.dot(normed, w_ref[...], preferred_element_type=F32).astype(BF16)


def norm_and_pairs(at, parts, gain, arrays):
    return pl.pallas_call(
        norm_kernel,
        out_shape=[
            jax.ShapeDtypeStruct((TOKENS, C), BF16),
            jax.ShapeDtypeStruct((TOKENS, C), BF16),
            jax.ShapeDtypeStruct((TOKENS, KV), BF16),
        ],
        in_specs=[SMEM] + [VMEM] * 5 + [ANY] * 2,
        out_specs=[VMEM] * 3,
        scratch_shapes=[pltpu.VMEM((C, KV), BF16), pltpu.SemaphoreType.DMA((16,))],
        compiler_params=params(20),
        cost_estimate=pl.CostEstimate(flops=2_000_000_000, bytes_accessed=3_500_000, transcendentals=0),
    )(at, *parts, gain, *arrays)


def query_kernel(at_ref, normed_ref, *refs):
    arrays, (out_ref, w_ref, sems) = refs[:2], refs[2:]
    wait_copies(place(at_ref, arrays, pl.ds(0, QW), w_ref, sems))
    queries = jnp.dot(normed_ref[...], w_ref[...], preferred_element_type=F32).astype(BF16)
    for head in range(HEADS):
        out_ref[head] = queries[:, head * HEAD_SIZE : (head + 1) * HEAD_SIZE]


def project_queries(at, normed, arrays):
    return pl.pallas_call(
        query_kernel,
        out_shape=jax.ShapeDtypeStruct((HEADS, TOKENS, HEAD_SIZE), BF16),
        in_specs=[SMEM, VMEM] + [ANY] * 2,
        out_specs=VMEM,
        scratch_shapes=[pltpu.VMEM((C, QW), BF16), pltpu.SemaphoreType.DMA((16,))],
        compiler_params=params(20),
        cost_estimate=pl.CostEstimate(flops=2_000_000_000, bytes_accessed=4_500_000, transcendentals=0),
    )(at, normed, *arrays)


def attend_head(head, scale_ref, q_ref, kvs, old_refs):
    scale = scale_ref[head]
    q = q_ref[head]
    lanes = (TOKENS, HEAD_SIZE)
    scores = [
        lax.dot_general(
            q, kv[:, :HEAD_SIZE], (((1,), (1,)), ((), ())), preferred_element_type=F32
        )
        for kv in kvs
    ]
    pieces = [
        [s[:, i : i + HEAD_SIZE] for i in range(0, s.shape[1], HEAD_SIZE)] for s in scores
    ]
    best = functools.reduce(jnp.maximum, [piece for group in pieces for piece in group])
    top = jnp.broadcast_to(jnp.max(best, axis=1, keepdims=True), lanes)
    if old_refs:
        old = old_refs[0][head]
        top = jnp.maximum(top, old)
        fade = jnp.exp2((old - top) * scale)
    total = jnp.zeros(lanes, F32)
    summed = jnp.zeros(lanes, F32)
    for group, kv in zip(pieces, kvs):
        weights = []
        for piece in group:
            e = jnp.exp2((piece - top) * scale)
            total = total + e
            weights.append(e.astype(BF16))
        summed = summed + jnp.dot(
            jnp.concatenate(weights, axis=1), kv[:, HEAD_SIZE:], preferred_element_type=F32
        )
    if old_refs:
        total = total + old_refs[1][head] * fade
        summed = summed + old_refs[2][head] * fade
    return top, total, summed


def attend_all(scale_ref, q_ref, kvs, old, new):
    @pl.loop(0, HEADS, step=4)
    def _(first):
        for i in range(4):
            for ref, value in zip(new, attend_head(first + i, scale_ref, q_ref, kvs, old)):
                ref[first + i] = value


def attend_kernel(n_blocks, scale_ref, q_ref, *refs):
    attend_all(scale_ref, q_ref, refs[:n_blocks], refs[n_blocks:-3], refs[-3:])


def attend(scale, queries, kvs, state):
    return pl.pallas_call(
        functools.partial(attend_kernel, len(kvs)),
        out_shape=[jax.ShapeDtypeStruct((HEADS, TOKENS, HEAD_SIZE), F32)] * 3,
        in_specs=[SMEM] + [VMEM] * (1 + len(kvs) + len(state)),
        out_specs=[VMEM] * 3,
        compiler_params=params(16),
        cost_estimate=pl.CostEstimate(flops=6_000_000_000, bytes_accessed=6_000_000, transcendentals=2_000_000),
    )(scale, queries, *kvs, *state)


def first_kernel(n_blocks, at_ref, scale_ref, q_ref, *refs):
    arrays, kvs, new, (w_ref, sems) = refs[:2], refs[2 : 2 + n_blocks], refs[2 + n_blocks : -2], refs[-2:]
    copies = place_out(at_ref, arrays, w_ref, sems)
    attend_all(scale_ref, q_ref, kvs, (), new)
    wait_copies(copies)


def attend_first(at, scale, queries, kvs, arrays):
    return pl.pallas_call(
        functools.partial(first_kernel, len(kvs)),
        out_shape=[jax.ShapeDtypeStruct((HEADS, TOKENS, HEAD_SIZE), F32)] * 3
        + [jax.ShapeDtypeStruct((QW, C), BF16)],
        in_specs=[SMEM, SMEM, VMEM, ANY, ANY] + [VMEM] * len(kvs),
        out_specs=[VMEM] * 4,
        scratch_shapes=[pltpu.SemaphoreType.DMA((48,))],
        compiler_params=params(16),
        cost_estimate=pl.CostEstimate(flops=6_000_000_000, bytes_accessed=9_000_000, transcendentals=2_000_000),
    )(at, scale, queries, *arrays, *kvs)


def out_kernel(total_ref, sum_ref, tokens_ref, w_ref, out_ref):
    heads = []
    for head in range(HEADS):
        total = jnp.sum(total_ref[head], axis=1, keepdims=True)
        heads.append((sum_ref[head] / total).astype(BF16))
    context = jnp.concatenate(heads, axis=1)
    update = jnp.dot(context, w_ref[...], preferred_element_type=F32)
    out_ref[...] = (update + tokens_ref[...].astype(F32)).astype(BF16)


def project_out(total, summed, tokens, weights):
    return pl.pallas_call(
        out_kernel,
        out_shape=jax.ShapeDtypeStruct((TOKENS, C), BF16),
        in_specs=[VMEM] * 4,
        out_specs=VMEM,
        compiler_params=params(24),
        cost_estimate=pl.CostEstimate(flops=2_000_000_000, bytes_accessed=7_000_000, transcendentals=0),
    )(total, summed, tokens, weights)


def on_device(
    dna_features, conv_weight, conv_bias, norm_gain, query_weight, kv_weight, out_weight, head_scale
):
    dp, seq = lax.axis_index("dp"), lax.axis_index("seq")
    core, z = dp % 2, seq % 8
    quarter = z % 2 * 2 + core
    at = jnp.stack([dp, quarter]).astype(jnp.int32)

    got = receive(conv_weight, from_core)
    start, shape = (0, 0, quarter * QUARTER), (KW, ROWS, QUARTER)
    keep, got = (lax.dynamic_slice(w, start, shape) for w in (conv_weight, got))
    unit = jnp.concatenate(
        [jnp.where(core == 0, keep, got), jnp.where(core == 0, got, keep)], axis=1
    )
    x1, x3, x2 = (receive(unit, from_x(step)) for step in (1, 3, 2))
    low, high = jnp.concatenate([unit, x1], axis=1), jnp.concatenate([x3, x2], axis=1)
    units = low, high, receive(low, from_y(1)), receive(high, from_y(-1))

    rows = dna_features.reshape(TOKENS, 2 * CIN)
    up = [(i, i + 1) for i in range(15)]
    ends = pack([rows[-1:], rows[:1]], [unit])
    before = lax.ppermute(ends[:, : 2 * CIN], "seq", up)
    behind = lax.ppermute(ends[:, 2 * CIN :], "seq", [(j, i) for i, j in up])
    rows = jnp.concatenate([before, rows, behind], axis=0)
    rows_z = receive(rows, from_z_pair)
    rows_c = receive(rows, from_core)
    rows_d = receive(rows_z, from_core)
    far, near = (
        jnp.stack([jnp.concatenate([r[:TOKENS], r[1 : TOKENS + 1], r[2:]], axis=1) for r in pair])
        for pair in ((rows_d, rows_z), (rows_c, rows))
    )
    bias = lax.dynamic_slice(conv_bias.reshape(1, C), (0, quarter * QUARTER), (1, QUARTER))

    projections = from_chips(pack_weights(query_weight, kv_weight, out_weight, high))
    t_d, t_z = convolve(at[:1] // 2, far, bias, units)
    t_c, t_own = convolve(at[:1] // 2, near, bias, units)
    got_z, got_d = receive(t_z, from_z_pair), receive(t_d, from_diagonal)
    projections, out_rows = stack(projections, [t_c, got_z, got_d])
    projections = projections, receive(projections, from_core)
    parts = t_own, receive(t_c, from_core), got_z, got_d
    tokens, normed, pairs = norm_and_pairs(at, parts, norm_gain.reshape(1, C), projections)

    out_rows = out_rows, receive(out_rows, from_core)
    queries = project_queries(at, normed, projections)
    scale = head_scale * (LOG2E / math.sqrt(HEAD_SIZE))

    both = jnp.concatenate([pairs, receive(pairs, from_y_hi)], axis=0)
    below, above = receive(both, from_z(-1)), receive(both, from_z(1))
    *state, out_weights = attend_first(at, scale, queries, [both, below, above], out_rows)
    for _ in range(2):
        below, above = receive(below, from_z(-1)), receive(above, from_z(1))
        state = attend(scale, queries, [below, above], state)
    last = [receive(below[:TOKENS], from_z(-1)), receive(above[TOKENS:], from_z(1))]
    state = attend(scale, queries, last, state)
    encoded = project_out(state[1], state[2], tokens, out_weights)
    return tokens[None], encoded[None]


def solution(mesh):
    in_specs = (
        P("dp", "seq", None),
        P(None, "dp", None),
        P(),
        P(),
        P("dp", None),
        P("dp", None),
        P("dp", None),
        P(),
    )
    out_specs = (P("dp", "seq", None), P("dp", "seq", None))
    return jax.shard_map(
        on_device, mesh=mesh, in_specs=in_specs, out_specs=out_specs, check_vma=False
    )
```

```python
import functools
import math

import jax
import jax.numpy as jnp
from jax import lax
from jax.experimental import pallas as pl
from jax.experimental.pallas import tpu as pltpu
from jax.sharding import PartitionSpec as P

CIN = 768
C = 1536
HEADS = 8
HEAD_SIZE = 128
KW = 5
QW = 1024
QUARTER = C // 4
TOKENS = 256
ROWS = CIN // 16
KV = 2 * HEAD_SIZE
BOTH = ("dp", "seq")
LOG2E = math.log2(math.e)
F32 = jnp.float32
BF16 = jnp.bfloat16


def places():
    for dp in range(16):
        for seq in range(16):
            yield dp // 4, dp // 2 % 2, dp % 2, seq // 8, seq % 8


def index(x, y_lo, core, y_hi, z):
    return (x * 4 + y_lo * 2 + core) * 16 + y_hi * 8 + z


def receive(value, source):
    pairs = [(index(*source(*p)), index(*p)) for p in places()]
    return lax.ppermute(value, BOTH, pairs)


def from_core(x, y, c, h, z):
    return x, y, 1 - c, h, z


def from_z_pair(x, y, c, h, z):
    return x, y, c, h, z ^ 1


def from_diagonal(x, y, c, h, z):
    return x, y, 1 - c, h, z ^ 1


def from_x(step):
    return lambda x, y, c, h, z: (x ^ step, y, c, h, z)


def from_y(step):
    def source(x, y, c, h, z):
        at = (h * 2 + y + step) % 4
        return x, at % 2, c, at // 2, z

    return source


def from_y_hi(x, y, c, h, z):
    return x, y, c, 1 - h, z


def from_z(step):
    return lambda x, y, c, h, z: (x, y, c, h, (z + step) % 8)


VMEM = pl.BlockSpec(memory_space=pltpu.VMEM)
SMEM = pl.BlockSpec(memory_space=pltpu.SMEM)
ANY = pl.BlockSpec(memory_space=pl.ANY)


def params(mib):
    return pltpu.CompilerParams(vmem_limit_bytes=mib * 2**20)


def start_copies(copies, sems):
    started = [pltpu.make_async_copy(a, b, sems.at[i]) for i, (a, b) in enumerate(copies)]
    for copy in started:
        copy.start()
    return started


def wait_copies(started):
    for copy in started:
        copy.wait()


def pack_kernel(n_weights, *refs):
    weights, packed_ref, start = refs[:n_weights], refs[-1], 0
    for weight in weights:
        packed_ref[:, start : start + weight.shape[1]] = weight[...]
        start += weight.shape[1]


def pack(weights, done):
    rows, columns = weights[0].shape[0], sum(w.shape[1] for w in weights)
    return pl.pallas_call(
        functools.partial(pack_kernel, len(weights)),
        out_shape=jax.ShapeDtypeStruct((rows, columns), BF16),
        in_specs=[VMEM] * len(weights) + [ANY] * len(done),
        out_specs=VMEM,
        compiler_params=params(8),
    )(*weights, *done)


def pack_weights_kernel(query_ref, kv_ref, out_ref, done_ref, packed_ref):
    packed_ref[:, :QW] = query_ref[...]
    packed_ref[:, QW : QW + KV] = kv_ref[...]
    packed_ref[: QW // 16, QW + KV :] = out_ref[:, :QW]
    packed_ref[QW // 16 :, QW + KV : QW + KV + 512] = out_ref[:32, QW:]
    packed_ref[QW // 16 :, QW + KV + 512 :] = out_ref[32:, QW:]


def pack_weights(query_weight, kv_weight, out_weight, done):
    return pl.pallas_call(
        pack_weights_kernel,
        out_shape=jax.ShapeDtypeStruct((C // 16, QW + KV + QW), BF16),
        in_specs=[VMEM] * 3 + [ANY],
        out_specs=VMEM,
        compiler_params=params(8),
    )(query_weight, kv_weight, out_weight, done)


CHIPS = (0, 2, 6, 4, 1, 3, 7, 5)


def stack_kernel(n_arrays, last, *refs):
    arrays, (out_ref, sems) = refs[:n_arrays], refs[-2:]
    rows, columns = arrays[0].shape[0], out_ref.shape[1]
    copies = []
    for i, array in enumerate(arrays):
        start = array.shape[1] - columns if last else 0
        copies.append((array.at[:, pl.ds(start, columns)], out_ref.at[pl.ds(i * rows, rows), :]))
    wait_copies(start_copies(copies, sems))


def stack(arrays, columns, done, last=False):
    rows = arrays[0].shape[0]
    return pl.pallas_call(
        functools.partial(stack_kernel, len(arrays), last),
        out_shape=jax.ShapeDtypeStruct((rows * len(arrays), columns), BF16),
        in_specs=[ANY] * (len(arrays) + len(done)),
        out_specs=VMEM,
        scratch_shapes=[pltpu.SemaphoreType.DMA((len(arrays),))],
        compiler_params=params(8),
    )(*arrays, *done)


def place(at_ref, arrays, columns, w_ref, sems):
    rows, copies = C // 16, []
    for core, array in enumerate(arrays):
        for slot, rel in enumerate(CHIPS):
            row = pl.multiple_of((at_ref[0] ^ (rel * 2 + core)) * rows, rows)
            copies.append((array.at[pl.ds(slot * rows, rows), columns], w_ref.at[pl.ds(row, rows), :]))
    return start_copies(copies, sems)


def place_out(at_ref, arrays, w_ref, sems):
    copies = []
    for core, array in enumerate(arrays):
        for slot, rel in enumerate(CHIPS):
            row = pl.multiple_of((at_ref[0] ^ (rel * 2 + core)) * 64, 64)
            late = pl.multiple_of(row + 32, 32)
            at, start = slot * 96, 0
            whole = array.at[pl.ds(at, 64), pl.ds(start, QW)]
            copies.append((whole, w_ref.at[pl.ds(row, 64), pl.ds(0, QW)]))
            for half, to in enumerate((row, late)):
                tail = array.at[pl.ds(at + 64, 32), pl.ds(start + half * 512, 512)]
                copies.append((tail, w_ref.at[pl.ds(to, 32), pl.ds(QW, 512)]))
    return start_copies(copies, sems)


def conv_blocks(a_ref, bias_ref, w_ref, outs):
    w = w_ref[...].reshape(KW * CIN, QUARTER)
    bias = bias_ref[...]
    even = jnp.dot(a_ref[0, :, : KW * CIN], w, preferred_element_type=F32) + bias
    odd = jnp.dot(a_ref[0, :, CIN:], w, preferred_element_type=F32) + bias
    pooled = jnp.maximum(jax.nn.gelu(even), jax.nn.gelu(odd)).astype(BF16)
    for i, out in enumerate(outs):

        @pl.when(pl.program_id(0) == i)
        def _(out=out):
            out[...] = pooled


def first_conv_kernel(at_ref, a_ref, bias_ref, *refs):
    units, outs, w_ref, sems = refs[:4], refs[4:6], refs[6], refs[7]

    @pl.when(pl.program_id(0) == 0)
    def _():
        copies = []
        for i, rel in enumerate(CHIPS):
            row = pl.multiple_of((at_ref[0] ^ rel) * (2 * ROWS), 2 * ROWS)
            unit = units[i // 2].at[:, pl.ds(i % 2 * 2 * ROWS, 2 * ROWS), :]
            copies.append((unit, w_ref.at[:, pl.ds(row, 2 * ROWS), :]))
        wait_copies(start_copies(copies, sems))

    conv_blocks(a_ref, bias_ref, w_ref, outs)


def conv_kernel(a_ref, bias_ref, w_ref, *outs):
    conv_blocks(a_ref, bias_ref, w_ref, outs)


CONV_COST = pl.CostEstimate(flops=8_000_000_000, bytes_accessed=8_000_000, transcendentals=393216)
BLOCK = pl.BlockSpec((1, TOKENS, 6 * CIN), lambda i: (i, 0, 0))
POOLED = [pl.BlockSpec((TOKENS, QUARTER), lambda i: (0, 0))] * 2
POOLED_SHAPE = [jax.ShapeDtypeStruct((TOKENS, QUARTER), BF16)] * 2


def convolve_first(chip, blocks, bias, units):
    return pl.pallas_call(
        first_conv_kernel,
        grid=(2,),
        out_shape=POOLED_SHAPE + [jax.ShapeDtypeStruct((KW, CIN, QUARTER), BF16)],
        in_specs=[SMEM, BLOCK, VMEM] + [ANY] * 4,
        out_specs=POOLED + [VMEM],
        scratch_shapes=[pltpu.SemaphoreType.DMA((8,))],
        compiler_params=params(24),
        cost_estimate=CONV_COST,
    )(chip, blocks, bias, *units)


def convolve(blocks, bias, whole):
    return pl.pallas_call(
        conv_kernel,
        grid=(2,),
        out_shape=POOLED_SHAPE,
        in_specs=[BLOCK, VMEM, VMEM],
        out_specs=POOLED,
        compiler_params=params(24),
        cost_estimate=CONV_COST,
    )(blocks, bias, whole)


def norm_kernel(at_ref, *refs):
    parts, gain_ref, arrays = refs[:4], refs[4], refs[5:7]
    tokens_ref, normed_ref, pairs_ref, w_ref, sems = refs[7:]
    copies = place(at_ref, arrays, pl.ds(QW, KV), w_ref, sems)
    for i, part in enumerate(parts):
        column = pl.multiple_of((at_ref[1] ^ i) * QUARTER, QUARTER)
        tokens_ref[:, pl.ds(column, QUARTER)] = part[...]
    wide = tokens_ref[...].astype(F32)
    stat = jnp.mean(jnp.square(wide), axis=-1, keepdims=True)
    normed = (wide * lax.rsqrt(stat + 1e-06) * gain_ref[...]).astype(BF16)
    normed_ref[...] = normed
    wait_copies(copies)
    pairs_ref[...] = jnp.dot(normed, w_ref[...], preferred_element_type=F32).astype(BF16)


def norm_and_pairs(at, parts, gain, arrays):
    return pl.pallas_call(
        norm_kernel,
        out_shape=[
            jax.ShapeDtypeStruct((TOKENS, C), BF16),
            jax.ShapeDtypeStruct((TOKENS, C), BF16),
            jax.ShapeDtypeStruct((TOKENS, KV), BF16),
        ],
        in_specs=[SMEM] + [VMEM] * 5 + [ANY] * 2,
        out_specs=[VMEM] * 3,
        scratch_shapes=[pltpu.VMEM((C, KV), BF16), pltpu.SemaphoreType.DMA((16,))],
        compiler_params=params(20),
        cost_estimate=pl.CostEstimate(flops=2_000_000_000, bytes_accessed=3_500_000, transcendentals=0),
    )(at, *parts, gain, *arrays)


def query_kernel(at_ref, normed_ref, *refs):
    arrays, (out_ref, w_ref, sems) = refs[:2], refs[2:]
    wait_copies(place(at_ref, arrays, pl.ds(0, QW), w_ref, sems))
    queries = jnp.dot(normed_ref[...], w_ref[...], preferred_element_type=F32).astype(BF16)
    for head in range(HEADS):
        out_ref[head] = queries[:, head * HEAD_SIZE : (head + 1) * HEAD_SIZE]


def project_queries(at, normed, arrays):
    return pl.pallas_call(
        query_kernel,
        out_shape=jax.ShapeDtypeStruct((HEADS, TOKENS, HEAD_SIZE), BF16),
        in_specs=[SMEM, VMEM] + [ANY] * 2,
        out_specs=VMEM,
        scratch_shapes=[pltpu.VMEM((C, QW), BF16), pltpu.SemaphoreType.DMA((16,))],
        compiler_params=params(20),
        cost_estimate=pl.CostEstimate(flops=2_000_000_000, bytes_accessed=4_500_000, transcendentals=0),
    )(at, normed, *arrays)


def attend_head(head, scale_ref, q_ref, kvs, old_refs):
    scale = scale_ref[head]
    q = q_ref[head]
    lanes = (TOKENS, HEAD_SIZE)
    scores = [
        lax.dot_general(
            q, kv[:, :HEAD_SIZE], (((1,), (1,)), ((), ())), preferred_element_type=F32
        )
        for kv in kvs
    ]
    pieces = [
        [s[:, i : i + HEAD_SIZE] for i in range(0, s.shape[1], HEAD_SIZE)] for s in scores
    ]
    best = functools.reduce(jnp.maximum, [piece for group in pieces for piece in group])
    top = jnp.broadcast_to(jnp.max(best, axis=1, keepdims=True), lanes)
    if old_refs:
        old = old_refs[0][head]
        top = jnp.maximum(top, old)
        fade = jnp.exp2((old - top) * scale)
    total = jnp.zeros(lanes, F32)
    summed = jnp.zeros(lanes, F32)
    for group, kv in zip(pieces, kvs):
        weights = []
        for piece in group:
            e = jnp.exp2((piece - top) * scale)
            total = total + e
            weights.append(e.astype(BF16))
        summed = summed + jnp.dot(
            jnp.concatenate(weights, axis=1), kv[:, HEAD_SIZE:], preferred_element_type=F32
        )
    if old_refs:
        total = total + old_refs[1][head] * fade
        summed = summed + old_refs[2][head] * fade
    return top, total, summed


def attend_all(scale_ref, q_ref, kvs, old, new):
    @pl.loop(0, HEADS, step=4)
    def _(first):
        for i in range(4):
            for ref, value in zip(new, attend_head(first + i, scale_ref, q_ref, kvs, old)):
                ref[first + i] = value


def attend_kernel(n_blocks, scale_ref, q_ref, *refs):
    attend_all(scale_ref, q_ref, refs[:n_blocks], refs[n_blocks:-3], refs[-3:])


def attend(scale, queries, kvs, state):
    return pl.pallas_call(
        functools.partial(attend_kernel, len(kvs)),
        out_shape=[jax.ShapeDtypeStruct((HEADS, TOKENS, HEAD_SIZE), F32)] * 3,
        in_specs=[SMEM] + [VMEM] * (1 + len(kvs) + len(state)),
        out_specs=[VMEM] * 3,
        compiler_params=params(16),
        cost_estimate=pl.CostEstimate(flops=6_000_000_000, bytes_accessed=6_000_000, transcendentals=2_000_000),
    )(scale, queries, *kvs, *state)


def place_kernel(n_blocks, at_ref, scale_ref, q_ref, *refs):
    arrays, kvs, refs = refs[:2], refs[2 : 2 + n_blocks], refs[2 + n_blocks :]
    old, new, w_ref, sems = refs[:3], refs[3:6], refs[6], refs[7]
    copies = place_out(at_ref, arrays, w_ref, sems)
    attend_all(scale_ref, q_ref, kvs, old, new)
    wait_copies(copies)


def attend_and_place(at, scale, queries, kvs, state, arrays):
    return pl.pallas_call(
        functools.partial(place_kernel, len(kvs)),
        out_shape=[jax.ShapeDtypeStruct((HEADS, TOKENS, HEAD_SIZE), F32)] * 3
        + [jax.ShapeDtypeStruct((QW, C), BF16)],
        in_specs=[SMEM, SMEM, VMEM, ANY, ANY] + [VMEM] * (len(kvs) + 3),
        out_specs=[VMEM] * 4,
        scratch_shapes=[pltpu.SemaphoreType.DMA((48,))],
        compiler_params=params(16),
        cost_estimate=pl.CostEstimate(flops=6_000_000_000, bytes_accessed=9_000_000, transcendentals=2_000_000),
    )(at, scale, queries, *arrays, *kvs, *state)


def out_kernel(total_ref, sum_ref, tokens_ref, w_ref, out_ref):
    heads = []
    for head in range(HEADS):
        total = jnp.sum(total_ref[head], axis=1, keepdims=True)
        heads.append((sum_ref[head] / total).astype(BF16))
    context = jnp.concatenate(heads, axis=1)
    update = jnp.dot(context, w_ref[...], preferred_element_type=F32)
    out_ref[...] = (update + tokens_ref[...].astype(F32)).astype(BF16)


def project_out(total, summed, tokens, weights):
    return pl.pallas_call(
        out_kernel,
        out_shape=jax.ShapeDtypeStruct((TOKENS, C), BF16),
        in_specs=[VMEM] * 4,
        out_specs=VMEM,
        compiler_params=params(24),
        cost_estimate=pl.CostEstimate(flops=2_000_000_000, bytes_accessed=7_000_000, transcendentals=0),
    )(total, summed, tokens, weights)


def on_device(
    dna_features, conv_weight, conv_bias, norm_gain, query_weight, kv_weight, out_weight, head_scale
):
    dp, seq = lax.axis_index("dp"), lax.axis_index("seq")
    core, z = dp % 2, seq % 8
    quarter = z % 2 * 2 + core
    at = jnp.stack([dp, quarter]).astype(jnp.int32)

    got = receive(conv_weight, from_core)
    start, shape = (0, 0, quarter * QUARTER), (KW, ROWS, QUARTER)
    keep, got = (lax.dynamic_slice(w, start, shape) for w in (conv_weight, got))
    unit = jnp.concatenate(
        [jnp.where(core == 0, keep, got), jnp.where(core == 0, got, keep)], axis=1
    )
    x1, x3, x2 = (receive(unit, from_x(step)) for step in (1, 3, 2))
    low, high = jnp.concatenate([unit, x1], axis=1), jnp.concatenate([x3, x2], axis=1)
    low_y = receive(low, from_y(1))
    units = low, high, low_y, receive(high, from_y(-1))

    even = z % 2 == 0
    rows = dna_features.reshape(TOKENS, 2 * CIN)
    rows_z = receive(rows, from_z_pair)
    edge = pack([jnp.where(even, rows[:1], rows[-1:])], [x1])
    beside = [p for i in range(1, 15, 2) for p in ((i, i + 1), (i + 1, i))]
    beyond = [(i, i - 2) for i in range(2, 16, 2)] + [(i, i + 2) for i in range(1, 14, 2)]
    beside, beyond = (lax.ppermute(edge, "seq", pairs) for pairs in (beside, beyond))

    def between(block, before, behind):
        return jnp.concatenate([before, block, behind], axis=0)

    pair_rows = between(
        rows_z, jnp.where(even, rows[-1:], beyond), jnp.where(even, beyond, rows[:1])
    )
    own_rows = between(
        rows, jnp.where(even, beside, rows_z[-1:]), jnp.where(even, rows_z[:1], beside)
    )
    far, near = (
        jnp.stack([jnp.concatenate([r[:TOKENS], r[1 : TOKENS + 1], r[2:]], axis=1) for r in pair])
        for pair in ((receive(pair_rows, from_core), pair_rows), (receive(own_rows, from_core), own_rows))
    )
    bias = lax.dynamic_slice(conv_bias.reshape(1, C), (0, quarter * QUARTER), (1, QUARTER))

    packed = pack_weights(query_weight, kv_weight, out_weight, high)
    px1, px3 = receive(packed, from_x(1)), receive(packed, from_x(3))
    low = jnp.concatenate([packed, px1], axis=0)
    high = jnp.concatenate([px3, receive(px3, from_x(1))], axis=0)
    high, high_out = high[:, : QW + KV], high[:, QW + KV :]
    projections = low, high, receive(low, from_y(1)), receive(high, from_y(-1))
    out_rows = low, high_out, projections[2], receive(high_out, from_y(-1))

    t_d, t_z, whole = convolve_first(at[:1] // 2, far, bias, units)
    got_z, got_d = receive(t_z, from_z_pair), receive(t_d, from_diagonal)
    t_c, t_own = convolve(near, bias, whole)
    projections = stack(projections, QW + KV, [t_c, got_z, got_d])
    projections = projections, receive(projections, from_core)
    parts = t_own, receive(t_c, from_core), got_z, got_d
    tokens, normed, pairs = norm_and_pairs(at, parts, norm_gain.reshape(1, C), projections)

    queries = project_queries(at, normed, projections)
    scale = head_scale * (LOG2E / math.sqrt(HEAD_SIZE))

    both = stack([pairs, receive(pairs, from_y_hi)], KV, [queries])
    below, above = receive(both, from_z(-1)), receive(both, from_z(1))
    out_rows = stack(out_rows, QW, [below, above], last=True)
    out_rows = out_rows, receive(out_rows, from_core)
    state = attend(scale, queries, [both, below, above], ())
    below, above = receive(below, from_z(-1)), receive(above, from_z(1))
    state = attend(scale, queries, [below, above], state)
    below, above = receive(below, from_z(-1)), receive(above, from_z(1))
    last = [receive(below[:TOKENS], from_z(-1)), receive(above[TOKENS:], from_z(1))]
    *state, out_weights = attend_and_place(at, scale, queries, [below, above], state, out_rows)
    state = attend(scale, queries, last, state)
    encoded = project_out(state[1], state[2], tokens, out_weights)
    return tokens[None], encoded[None]


def solution(mesh):
    in_specs = (
        P("dp", "seq", None),
        P(None, "dp", None),
        P(),
        P(),
        P("dp", None),
        P("dp", None),
        P("dp", None),
        P(),
    )
    out_specs = (P("dp", "seq", None), P("dp", "seq", None))
    return jax.shard_map(
        on_device, mesh=mesh, in_specs=in_specs, out_specs=out_specs, check_vma=False
    )
```

```python
import functools
import math

import jax
import jax.numpy as jnp
from jax import lax
from jax.experimental import pallas as pl
from jax.experimental.pallas import tpu as pltpu
from jax.sharding import PartitionSpec as P

CIN = 768
C = 1536
HEADS = 8
HEAD_SIZE = 128
KW = 5
QW = 1024
QUARTER = C // 4
TOKENS = 256
ROWS = CIN // 16
KV = 2 * HEAD_SIZE
BOTH = ("dp", "seq")
LOG2E = math.log2(math.e)
F32 = jnp.float32
BF16 = jnp.bfloat16


def places():
    for dp in range(16):
        for seq in range(16):
            yield dp // 4, dp // 2 % 2, dp % 2, seq // 8, seq % 8


def index(x, y_lo, core, y_hi, z):
    return (x * 4 + y_lo * 2 + core) * 16 + y_hi * 8 + z


def receive(value, source):
    pairs = [(index(*source(*p)), index(*p)) for p in places()]
    return lax.ppermute(value, BOTH, pairs)


def from_core(x, y, c, h, z):
    return x, y, 1 - c, h, z


def from_z_pair(x, y, c, h, z):
    return x, y, c, h, z ^ 1


def from_diagonal(x, y, c, h, z):
    return x, y, 1 - c, h, z ^ 1


def from_x(step):
    return lambda x, y, c, h, z: (x ^ step, y, c, h, z)


def from_y(step):
    def source(x, y, c, h, z):
        at = (h * 2 + y + step) % 4
        return x, at % 2, c, at // 2, z

    return source


def from_y_hi(x, y, c, h, z):
    return x, y, c, 1 - h, z


def from_z(step):
    return lambda x, y, c, h, z: (x, y, c, h, (z + step) % 8)


VMEM = pl.BlockSpec(memory_space=pltpu.VMEM)
SMEM = pl.BlockSpec(memory_space=pltpu.SMEM)
ANY = pl.BlockSpec(memory_space=pl.ANY)


def params(mib):
    return pltpu.CompilerParams(vmem_limit_bytes=mib * 2**20)


def start_copies(copies, sems):
    started = [pltpu.make_async_copy(a, b, sems.at[i]) for i, (a, b) in enumerate(copies)]
    for copy in started:
        copy.start()
    return started


def wait_copies(started):
    for copy in started:
        copy.wait()


def pack_kernel(n_weights, *refs):
    weights, packed_ref, start = refs[:n_weights], refs[-1], 0
    for weight in weights:
        packed_ref[:, start : start + weight.shape[1]] = weight[...]
        start += weight.shape[1]


def pack(weights, done):
    rows, columns = weights[0].shape[0], sum(w.shape[1] for w in weights)
    return pl.pallas_call(
        functools.partial(pack_kernel, len(weights)),
        out_shape=jax.ShapeDtypeStruct((rows, columns), BF16),
        in_specs=[VMEM] * len(weights) + [ANY] * len(done),
        out_specs=VMEM,
        compiler_params=params(8),
    )(*weights, *done)


def pack_weights_kernel(query_ref, kv_ref, out_ref, done_ref, packed_ref):
    packed_ref[:, :QW] = query_ref[...]
    packed_ref[:, QW : QW + KV] = kv_ref[...]
    packed_ref[: QW // 16, QW + KV :] = out_ref[:, :QW]
    packed_ref[QW // 16 :, QW + KV : QW + KV + 512] = out_ref[:32, QW:]
    packed_ref[QW // 16 :, QW + KV + 512 :] = out_ref[32:, QW:]


def pack_weights(query_weight, kv_weight, out_weight, done):
    return pl.pallas_call(
        pack_weights_kernel,
        out_shape=jax.ShapeDtypeStruct((C // 16, QW + KV + QW), BF16),
        in_specs=[VMEM] * 3 + [ANY],
        out_specs=VMEM,
        compiler_params=params(8),
    )(query_weight, kv_weight, out_weight, done)


CHIPS = (0, 2, 6, 4, 1, 3, 7, 5)


def stack_kernel(n_arrays, last, *refs):
    arrays, (out_ref, sems) = refs[:n_arrays], refs[-2:]
    columns, row, copies = out_ref.shape[1], 0, []
    for array in arrays:
        rows, start = array.shape[0], array.shape[1] - columns if last else 0
        copies.append((array.at[:, pl.ds(start, columns)], out_ref.at[pl.ds(row, rows), :]))
        row += rows
    wait_copies(start_copies(copies, sems))


def stack(arrays, columns, done, last=False):
    rows = sum(array.shape[0] for array in arrays)
    return pl.pallas_call(
        functools.partial(stack_kernel, len(arrays), last),
        out_shape=jax.ShapeDtypeStruct((rows, columns), BF16),
        in_specs=[ANY] * (len(arrays) + len(done)),
        out_specs=VMEM,
        scratch_shapes=[pltpu.SemaphoreType.DMA((len(arrays),))],
        compiler_params=params(8),
    )(*arrays, *done)


def place(at_ref, arrays, columns, w_ref, sems):
    rows, copies = C // 16, []
    for core, array in enumerate(arrays):
        for slot, rel in enumerate(CHIPS):
            row = pl.multiple_of((at_ref[0] ^ (rel * 2 + core)) * rows, rows)
            copies.append((array.at[pl.ds(slot * rows, rows), columns], w_ref.at[pl.ds(row, rows), :]))
    return start_copies(copies, sems)


def place_out(at_ref, arrays, w_ref, sems):
    copies = []
    for core, array in enumerate(arrays):
        for slot, rel in enumerate(CHIPS):
            row = pl.multiple_of((at_ref[0] ^ (rel * 2 + core)) * 64, 64)
            late = pl.multiple_of(row + 32, 32)
            at, start = slot * 96, 0
            whole = array.at[pl.ds(at, 64), pl.ds(start, QW)]
            copies.append((whole, w_ref.at[pl.ds(row, 64), pl.ds(0, QW)]))
            for half, to in enumerate((row, late)):
                tail = array.at[pl.ds(at + 64, 32), pl.ds(start + half * 512, 512)]
                copies.append((tail, w_ref.at[pl.ds(to, 32), pl.ds(QW, 512)]))
    return start_copies(copies, sems)


def conv_blocks(a_ref, bias_ref, w_ref, outs):
    w = w_ref[...].reshape(KW * CIN, QUARTER)
    bias = bias_ref[...]
    even = jnp.dot(a_ref[0, :, : KW * CIN], w, preferred_element_type=F32) + bias
    odd = jnp.dot(a_ref[0, :, CIN:], w, preferred_element_type=F32) + bias
    pooled = jnp.maximum(jax.nn.gelu(even), jax.nn.gelu(odd)).astype(BF16)
    for i, out in enumerate(outs):

        @pl.when(pl.program_id(0) == i)
        def _(out=out):
            out[...] = pooled


def first_conv_kernel(at_ref, a_ref, bias_ref, *refs):
    units, outs, w_ref, sems = refs[:4], refs[4:6], refs[6], refs[7]

    @pl.when(pl.program_id(0) == 0)
    def _():
        copies = []
        for i, rel in enumerate(CHIPS):
            row = pl.multiple_of((at_ref[0] ^ rel) * (2 * ROWS), 2 * ROWS)
            unit = units[i // 2].at[:, pl.ds(i % 2 * 2 * ROWS, 2 * ROWS), :]
            copies.append((unit, w_ref.at[:, pl.ds(row, 2 * ROWS), :]))
        wait_copies(start_copies(copies, sems))

    conv_blocks(a_ref, bias_ref, w_ref, outs)


def conv_kernel(a_ref, bias_ref, w_ref, *outs):
    conv_blocks(a_ref, bias_ref, w_ref, outs)


CONV_COST = pl.CostEstimate(flops=8_000_000_000, bytes_accessed=8_000_000, transcendentals=393216)
BLOCK = pl.BlockSpec((1, TOKENS, 6 * CIN), lambda i: (i, 0, 0))
POOLED = [pl.BlockSpec((TOKENS, QUARTER), lambda i: (0, 0))] * 2
POOLED_SHAPE = [jax.ShapeDtypeStruct((TOKENS, QUARTER), BF16)] * 2


def convolve_first(chip, blocks, bias, units):
    return pl.pallas_call(
        first_conv_kernel,
        grid=(2,),
        out_shape=POOLED_SHAPE + [jax.ShapeDtypeStruct((KW, CIN, QUARTER), BF16)],
        in_specs=[SMEM, BLOCK, VMEM] + [ANY] * 4,
        out_specs=POOLED + [VMEM],
        scratch_shapes=[pltpu.SemaphoreType.DMA((8,))],
        compiler_params=params(24),
        cost_estimate=CONV_COST,
    )(chip, blocks, bias, *units)


def convolve(blocks, bias, whole):
    return pl.pallas_call(
        conv_kernel,
        grid=(2,),
        out_shape=POOLED_SHAPE,
        in_specs=[BLOCK, VMEM, VMEM],
        out_specs=POOLED,
        compiler_params=params(24),
        cost_estimate=CONV_COST,
    )(blocks, bias, whole)


def norm_kernel(at_ref, *refs):
    parts, gain_ref, arrays = refs[:4], refs[4], refs[5:7]
    tokens_ref, normed_ref, pairs_ref, w_ref, sems = refs[7:]
    copies = place(at_ref, arrays, pl.ds(QW, KV), w_ref, sems)
    for i, part in enumerate(parts):
        column = pl.multiple_of((at_ref[1] ^ i) * QUARTER, QUARTER)
        tokens_ref[:, pl.ds(column, QUARTER)] = part[...]
    wide = tokens_ref[...].astype(F32)
    stat = jnp.mean(jnp.square(wide), axis=-1, keepdims=True)
    normed = (wide * lax.rsqrt(stat + 1e-06) * gain_ref[...]).astype(BF16)
    normed_ref[...] = normed
    wait_copies(copies)
    pairs_ref[...] = jnp.dot(normed, w_ref[...], preferred_element_type=F32).astype(BF16)


def norm_and_pairs(at, parts, gain, arrays):
    return pl.pallas_call(
        norm_kernel,
        out_shape=[
            jax.ShapeDtypeStruct((TOKENS, C), BF16),
            jax.ShapeDtypeStruct((TOKENS, C), BF16),
            jax.ShapeDtypeStruct((TOKENS, KV), BF16),
        ],
        in_specs=[SMEM] + [VMEM] * 5 + [ANY] * 2,
        out_specs=[VMEM] * 3,
        scratch_shapes=[pltpu.VMEM((C, KV), BF16), pltpu.SemaphoreType.DMA((16,))],
        compiler_params=params(20),
        cost_estimate=pl.CostEstimate(flops=2_000_000_000, bytes_accessed=3_500_000, transcendentals=0),
    )(at, *parts, gain, *arrays)


def query_kernel(at_ref, normed_ref, *refs):
    arrays, (out_ref, w_ref, sems) = refs[:2], refs[2:]
    wait_copies(place(at_ref, arrays, pl.ds(0, QW), w_ref, sems))
    queries = jnp.dot(normed_ref[...], w_ref[...], preferred_element_type=F32).astype(BF16)
    for head in range(HEADS):
        out_ref[head] = queries[:, head * HEAD_SIZE : (head + 1) * HEAD_SIZE]


def project_queries(at, normed, arrays):
    return pl.pallas_call(
        query_kernel,
        out_shape=jax.ShapeDtypeStruct((HEADS, TOKENS, HEAD_SIZE), BF16),
        in_specs=[SMEM, VMEM] + [ANY] * 2,
        out_specs=VMEM,
        scratch_shapes=[pltpu.VMEM((C, QW), BF16), pltpu.SemaphoreType.DMA((16,))],
        compiler_params=params(20),
        cost_estimate=pl.CostEstimate(flops=2_000_000_000, bytes_accessed=4_500_000, transcendentals=0),
    )(at, normed, *arrays)


def attend_head(head, scale_ref, q_ref, kvs, old_refs):
    scale = scale_ref[head]
    q = q_ref[head]
    lanes = (TOKENS, HEAD_SIZE)
    scores = [
        lax.dot_general(
            q, kv[:, :HEAD_SIZE], (((1,), (1,)), ((), ())), preferred_element_type=F32
        )
        for kv in kvs
    ]
    pieces = [
        [s[:, i : i + HEAD_SIZE] for i in range(0, s.shape[1], HEAD_SIZE)] for s in scores
    ]
    best = functools.reduce(jnp.maximum, [piece for group in pieces for piece in group])
    top = jnp.broadcast_to(jnp.max(best, axis=1, keepdims=True), lanes)
    if old_refs:
        old = old_refs[0][head]
        top = jnp.maximum(top, old)
        fade = jnp.exp2((old - top) * scale)
    total = jnp.zeros(lanes, F32)
    summed = jnp.zeros(lanes, F32)
    for group, kv in zip(pieces, kvs):
        weights = []
        for piece in group:
            e = jnp.exp2((piece - top) * scale)
            total = total + e
            weights.append(e.astype(BF16))
        summed = summed + jnp.dot(
            jnp.concatenate(weights, axis=1), kv[:, HEAD_SIZE:], preferred_element_type=F32
        )
    if old_refs:
        total = total + old_refs[1][head] * fade
        summed = summed + old_refs[2][head] * fade
    return top, total, summed


def attend_all(scale_ref, q_ref, kvs, old, new):
    @pl.loop(0, HEADS, step=4)
    def _(first):
        for i in range(4):
            for ref, value in zip(new, attend_head(first + i, scale_ref, q_ref, kvs, old)):
                ref[first + i] = value


def attend_kernel(n_blocks, scale_ref, q_ref, *refs):
    attend_all(scale_ref, q_ref, refs[:n_blocks], refs[n_blocks:-3], refs[-3:])


def attend(scale, queries, kvs, state):
    return pl.pallas_call(
        functools.partial(attend_kernel, len(kvs)),
        out_shape=[jax.ShapeDtypeStruct((HEADS, TOKENS, HEAD_SIZE), F32)] * 3,
        in_specs=[SMEM] + [VMEM] * (1 + len(kvs) + len(state)),
        out_specs=[VMEM] * 3,
        compiler_params=params(16),
        cost_estimate=pl.CostEstimate(flops=6_000_000_000, bytes_accessed=6_000_000, transcendentals=2_000_000),
    )(scale, queries, *kvs, *state)


def place_kernel(n_blocks, at_ref, scale_ref, q_ref, *refs):
    arrays, kvs, refs = refs[:2], refs[2 : 2 + n_blocks], refs[2 + n_blocks :]
    old, new, w_ref, sems = refs[:3], refs[3:6], refs[6], refs[7]
    copies = place_out(at_ref, arrays, w_ref, sems)
    attend_all(scale_ref, q_ref, kvs, old, new)
    wait_copies(copies)


def attend_and_place(at, scale, queries, kvs, state, arrays):
    return pl.pallas_call(
        functools.partial(place_kernel, len(kvs)),
        out_shape=[jax.ShapeDtypeStruct((HEADS, TOKENS, HEAD_SIZE), F32)] * 3
        + [jax.ShapeDtypeStruct((QW, C), BF16)],
        in_specs=[SMEM, SMEM, VMEM, ANY, ANY] + [VMEM] * (len(kvs) + 3),
        out_specs=[VMEM] * 4,
        scratch_shapes=[pltpu.SemaphoreType.DMA((48,))],
        compiler_params=params(16),
        cost_estimate=pl.CostEstimate(flops=6_000_000_000, bytes_accessed=9_000_000, transcendentals=2_000_000),
    )(at, scale, queries, *arrays, *kvs, *state)


def out_kernel(total_ref, sum_ref, tokens_ref, w_ref, out_ref):
    heads = []
    for head in range(HEADS):
        total = jnp.sum(total_ref[head], axis=1, keepdims=True)
        heads.append((sum_ref[head] / total).astype(BF16))
    context = jnp.concatenate(heads, axis=1)
    update = jnp.dot(context, w_ref[...], preferred_element_type=F32)
    out_ref[...] = (update + tokens_ref[...].astype(F32)).astype(BF16)


def project_out(total, summed, tokens, weights):
    return pl.pallas_call(
        out_kernel,
        out_shape=jax.ShapeDtypeStruct((TOKENS, C), BF16),
        in_specs=[VMEM] * 4,
        out_specs=VMEM,
        compiler_params=params(24),
        cost_estimate=pl.CostEstimate(flops=2_000_000_000, bytes_accessed=7_000_000, transcendentals=0),
    )(total, summed, tokens, weights)


def on_device(
    dna_features, conv_weight, conv_bias, norm_gain, query_weight, kv_weight, out_weight, head_scale
):
    dp, seq = lax.axis_index("dp"), lax.axis_index("seq")
    core, z = dp % 2, seq % 8
    quarter = z % 2 * 2 + core
    at = jnp.stack([dp, quarter]).astype(jnp.int32)

    got = receive(conv_weight, from_core)
    start, shape = (0, 0, quarter * QUARTER), (KW, ROWS, QUARTER)
    keep, got = (lax.dynamic_slice(w, start, shape) for w in (conv_weight, got))
    unit = jnp.concatenate(
        [jnp.where(core == 0, keep, got), jnp.where(core == 0, got, keep)], axis=1
    )
    x1, x3, x2 = (receive(unit, from_x(step)) for step in (1, 3, 2))
    low, high = jnp.concatenate([unit, x1], axis=1), jnp.concatenate([x3, x2], axis=1)
    low_y = receive(low, from_y(1))
    units = low, high, low_y, receive(high, from_y(-1))

    even = z % 2 == 0
    rows = dna_features.reshape(TOKENS, 2 * CIN)
    rows_z = receive(rows, from_z_pair)
    edge = pack([jnp.where(even, rows[:1], rows[-1:])], [x1])
    beside = [p for i in range(1, 15, 2) for p in ((i, i + 1), (i + 1, i))]
    beyond = [(i, i - 2) for i in range(2, 16, 2)] + [(i, i + 2) for i in range(1, 14, 2)]
    beside, beyond = (lax.ppermute(edge, "seq", pairs) for pairs in (beside, beyond))

    def between(block, before, behind):
        return jnp.concatenate([before, block, behind], axis=0)

    pair_rows = between(
        rows_z, jnp.where(even, rows[-1:], beyond), jnp.where(even, beyond, rows[:1])
    )
    own_rows = between(
        rows, jnp.where(even, beside, rows_z[-1:]), jnp.where(even, rows_z[:1], beside)
    )
    far, near = (
        jnp.stack([jnp.concatenate([r[:TOKENS], r[1 : TOKENS + 1], r[2:]], axis=1) for r in pair])
        for pair in ((receive(pair_rows, from_core), pair_rows), (receive(own_rows, from_core), own_rows))
    )
    bias = lax.dynamic_slice(conv_bias.reshape(1, C), (0, quarter * QUARTER), (1, QUARTER))

    packed = pack_weights(query_weight, kv_weight, out_weight, high)
    px1, px3 = receive(packed, from_x(1)), receive(packed, from_x(3))
    low = jnp.concatenate([packed, px1], axis=0)
    low_y = receive(low, from_y(1))
    px2 = receive(px3, from_x(1))
    py3, py2 = (receive(rows[:, : QW + KV], from_y(-1)) for rows in (px3, px2))
    projections = low, px3, px2, low_y, py3, py2
    high_out = jnp.concatenate([px3[:, QW + KV :], px2[:, QW + KV :]], axis=0)
    out_rows = low, high_out, low_y, receive(high_out, from_y(-1))

    t_d, t_z, whole = convolve_first(at[:1] // 2, far, bias, units)
    got_z, got_d = receive(t_z, from_z_pair), receive(t_d, from_diagonal)
    t_c, t_own = convolve(near, bias, whole)
    projections = stack(projections, QW + KV, [t_c, got_z, got_d])
    projections = projections, receive(projections, from_core)
    parts = t_own, receive(t_c, from_core), got_z, got_d
    tokens, normed, pairs = norm_and_pairs(at, parts, norm_gain.reshape(1, C), projections)

    queries = project_queries(at, normed, projections)
    scale = head_scale * (LOG2E / math.sqrt(HEAD_SIZE))

    both = stack([pairs, receive(pairs, from_y_hi)], KV, [queries])
    below, above = receive(both, from_z(-1)), receive(both, from_z(1))
    out_rows = stack(out_rows, QW, [below, above], last=True)
    out_rows = out_rows, receive(out_rows, from_core)
    state = attend(scale, queries, [both, below, above], ())
    below, above = receive(below, from_z(-1)), receive(above, from_z(1))
    state = attend(scale, queries, [below, above], state)
    below, above = receive(below, from_z(-1)), receive(above, from_z(1))
    last = [receive(below[:TOKENS], from_z(-1)), receive(above[TOKENS:], from_z(1))]
    *state, out_weights = attend_and_place(at, scale, queries, [below, above], state, out_rows)
    state = attend(scale, queries, last, state)
    encoded = project_out(state[1], state[2], tokens, out_weights)
    return tokens[None], encoded[None]


def solution(mesh):
    in_specs = (
        P("dp", "seq", None),
        P(None, "dp", None),
        P(),
        P(),
        P("dp", None),
        P("dp", None),
        P("dp", None),
        P(),
    )
    out_specs = (P("dp", "seq", None), P("dp", "seq", None))
    return jax.shard_map(
        on_device, mesh=mesh, in_specs=in_specs, out_specs=out_specs, check_vma=False
    )
```

```python
import functools
import math

import jax
import jax.numpy as jnp
from jax import lax
from jax.experimental import pallas as pl
from jax.experimental.pallas import tpu as pltpu
from jax.sharding import PartitionSpec as P

CIN = 768
C = 1536
HEADS = 8
HEAD_SIZE = 128
KW = 5
QW = 1024
QUARTER = C // 4
TOKENS = 256
ROWS = CIN // 16
KV = 2 * HEAD_SIZE
BOTH = ("dp", "seq")
LOG2E = math.log2(math.e)
F32 = jnp.float32
BF16 = jnp.bfloat16


def places():
    for dp in range(16):
        for seq in range(16):
            yield dp // 4, dp // 2 % 2, dp % 2, seq // 8, seq % 8


def index(x, y_lo, core, y_hi, z):
    return (x * 4 + y_lo * 2 + core) * 16 + y_hi * 8 + z


def receive(value, source):
    pairs = [(index(*source(*p)), index(*p)) for p in places()]
    return lax.ppermute(value, BOTH, pairs)


def from_core(x, y, c, h, z):
    return x, y, 1 - c, h, z


def from_z_pair(x, y, c, h, z):
    return x, y, c, h, z ^ 1


def from_diagonal(x, y, c, h, z):
    return x, y, 1 - c, h, z ^ 1


def from_x(step):
    return lambda x, y, c, h, z: (x ^ step, y, c, h, z)


def from_y(step):
    def source(x, y, c, h, z):
        at = (h * 2 + y + step) % 4
        return x, at % 2, c, at // 2, z

    return source


def from_y_hi(x, y, c, h, z):
    return x, y, c, 1 - h, z


def from_z(step):
    return lambda x, y, c, h, z: (x, y, c, h, (z + step) % 8)


VMEM = pl.BlockSpec(memory_space=pltpu.VMEM)
SMEM = pl.BlockSpec(memory_space=pltpu.SMEM)
ANY = pl.BlockSpec(memory_space=pl.ANY)


def params(mib):
    return pltpu.CompilerParams(vmem_limit_bytes=mib * 2**20)


def start_copies(copies, sems):
    started = [pltpu.make_async_copy(a, b, sems.at[i]) for i, (a, b) in enumerate(copies)]
    for copy in started:
        copy.start()
    return started


def wait_copies(started):
    for copy in started:
        copy.wait()


def pack_kernel(n_weights, *refs):
    weights, packed_ref, start = refs[:n_weights], refs[-1], 0
    for weight in weights:
        packed_ref[:, start : start + weight.shape[1]] = weight[...]
        start += weight.shape[1]


def pack(weights, done):
    rows, columns = weights[0].shape[0], sum(w.shape[1] for w in weights)
    return pl.pallas_call(
        functools.partial(pack_kernel, len(weights)),
        out_shape=jax.ShapeDtypeStruct((rows, columns), BF16),
        in_specs=[VMEM] * len(weights) + [ANY] * len(done),
        out_specs=VMEM,
        compiler_params=params(8),
    )(*weights, *done)


def pack_weights_kernel(query_ref, kv_ref, out_ref, done_ref, packed_ref):
    packed_ref[:, :QW] = query_ref[...]
    packed_ref[:, QW : QW + KV] = kv_ref[...]
    packed_ref[: QW // 16, QW + KV :] = out_ref[:, :QW]
    packed_ref[QW // 16 :, QW + KV : QW + KV + 512] = out_ref[:32, QW:]
    packed_ref[QW // 16 :, QW + KV + 512 :] = out_ref[32:, QW:]


def pack_weights(query_weight, kv_weight, out_weight, done):
    return pl.pallas_call(
        pack_weights_kernel,
        out_shape=jax.ShapeDtypeStruct((C // 16, QW + KV + QW), BF16),
        in_specs=[VMEM] * 3 + [ANY],
        out_specs=VMEM,
        compiler_params=params(8),
    )(query_weight, kv_weight, out_weight, done)


CHIPS = (0, 2, 6, 4, 1, 3, 7, 5)


def stack_kernel(n_arrays, last, *refs):
    arrays, (out_ref, sems) = refs[:n_arrays], refs[-2:]
    columns, row, copies = out_ref.shape[1], 0, []
    for array in arrays:
        rows, start = array.shape[0], array.shape[1] - columns if last else 0
        copies.append((array.at[:, pl.ds(start, columns)], out_ref.at[pl.ds(row, rows), :]))
        row += rows
    wait_copies(start_copies(copies, sems))


def stack(arrays, columns, done, last=False):
    rows = sum(array.shape[0] for array in arrays)
    return pl.pallas_call(
        functools.partial(stack_kernel, len(arrays), last),
        out_shape=jax.ShapeDtypeStruct((rows, columns), BF16),
        in_specs=[ANY] * (len(arrays) + len(done)),
        out_specs=VMEM,
        scratch_shapes=[pltpu.SemaphoreType.DMA((len(arrays),))],
        compiler_params=params(8),
    )(*arrays, *done)


def place(at_ref, arrays, columns, w_ref, sems):
    rows, copies = C // 16, []
    for core, array in enumerate(arrays):
        for slot, rel in enumerate(CHIPS):
            row = pl.multiple_of((at_ref[0] ^ (rel * 2 + core)) * rows, rows)
            copies.append((array.at[pl.ds(slot * rows, rows), columns], w_ref.at[pl.ds(row, rows), :]))
    return start_copies(copies, sems)


def place_out(at_ref, arrays, w_ref, sems):
    copies = []
    for core, array in enumerate(arrays):
        for slot, rel in enumerate(CHIPS):
            row = pl.multiple_of((at_ref[0] ^ (rel * 2 + core)) * 64, 64)
            late = pl.multiple_of(row + 32, 32)
            at, start = slot * 96, 0
            whole = array.at[pl.ds(at, 64), pl.ds(start, QW)]
            copies.append((whole, w_ref.at[pl.ds(row, 64), pl.ds(0, QW)]))
            for half, to in enumerate((row, late)):
                tail = array.at[pl.ds(at + 64, 32), pl.ds(start + half * 512, 512)]
                copies.append((tail, w_ref.at[pl.ds(to, 32), pl.ds(QW, 512)]))
    return start_copies(copies, sems)


def conv_blocks(a_ref, bias_ref, w_ref, outs):
    w = w_ref[...].reshape(KW * CIN, QUARTER)
    bias = bias_ref[...]
    even = jnp.dot(a_ref[0, :, : KW * CIN], w, preferred_element_type=F32) + bias
    odd = jnp.dot(a_ref[0, :, CIN:], w, preferred_element_type=F32) + bias
    pooled = jnp.maximum(jax.nn.gelu(even), jax.nn.gelu(odd)).astype(BF16)
    for i, out in enumerate(outs):

        @pl.when(pl.program_id(0) == i)
        def _(out=out):
            out[...] = pooled


def first_conv_kernel(at_ref, a_ref, bias_ref, *refs):
    units, outs, w_ref, sems = refs[:4], refs[4:6], refs[6], refs[7]

    @pl.when(pl.program_id(0) == 0)
    def _():
        copies = []
        for i, rel in enumerate(CHIPS):
            row = pl.multiple_of((at_ref[0] ^ rel) * (2 * ROWS), 2 * ROWS)
            unit = units[i // 2].at[:, pl.ds(i % 2 * 2 * ROWS, 2 * ROWS), :]
            copies.append((unit, w_ref.at[:, pl.ds(row, 2 * ROWS), :]))
        wait_copies(start_copies(copies, sems))

    conv_blocks(a_ref, bias_ref, w_ref, outs)


def conv_kernel(a_ref, bias_ref, w_ref, *outs):
    conv_blocks(a_ref, bias_ref, w_ref, outs)


CONV_COST = pl.CostEstimate(flops=8_000_000_000, bytes_accessed=8_000_000, transcendentals=393216)
BLOCK = pl.BlockSpec((1, TOKENS, 6 * CIN), lambda i: (i, 0, 0))
POOLED = [pl.BlockSpec((TOKENS, QUARTER), lambda i: (0, 0))] * 2
POOLED_SHAPE = [jax.ShapeDtypeStruct((TOKENS, QUARTER), BF16)] * 2


def convolve_first(chip, blocks, bias, units):
    return pl.pallas_call(
        first_conv_kernel,
        grid=(2,),
        out_shape=POOLED_SHAPE + [jax.ShapeDtypeStruct((KW, CIN, QUARTER), BF16)],
        in_specs=[SMEM, BLOCK, VMEM] + [ANY] * 4,
        out_specs=POOLED + [VMEM],
        scratch_shapes=[pltpu.SemaphoreType.DMA((8,))],
        compiler_params=params(24),
        cost_estimate=CONV_COST,
    )(chip, blocks, bias, *units)


def convolve(blocks, bias, whole):
    return pl.pallas_call(
        conv_kernel,
        grid=(2,),
        out_shape=POOLED_SHAPE,
        in_specs=[BLOCK, VMEM, VMEM],
        out_specs=POOLED,
        compiler_params=params(24),
        cost_estimate=CONV_COST,
    )(blocks, bias, whole)


def norm_kernel(at_ref, *refs):
    parts, gain_ref, arrays = refs[:4], refs[4], refs[5:7]
    tokens_ref, normed_ref, pairs_ref, w_ref, sems = refs[7:]
    copies = place(at_ref, arrays, pl.ds(QW, KV), w_ref, sems)
    for i, part in enumerate(parts):
        column = pl.multiple_of((at_ref[1] ^ i) * QUARTER, QUARTER)
        tokens_ref[:, pl.ds(column, QUARTER)] = part[...]
    wide = tokens_ref[...].astype(F32)
    stat = jnp.mean(jnp.square(wide), axis=-1, keepdims=True)
    normed = (wide * lax.rsqrt(stat + 1e-06) * gain_ref[...]).astype(BF16)
    normed_ref[...] = normed
    wait_copies(copies)
    pairs_ref[...] = jnp.dot(normed, w_ref[...], preferred_element_type=F32).astype(BF16)


def norm_and_pairs(at, parts, gain, arrays):
    return pl.pallas_call(
        norm_kernel,
        out_shape=[
            jax.ShapeDtypeStruct((TOKENS, C), BF16),
            jax.ShapeDtypeStruct((TOKENS, C), BF16),
            jax.ShapeDtypeStruct((TOKENS, KV), BF16),
        ],
        in_specs=[SMEM] + [VMEM] * 5 + [ANY] * 2,
        out_specs=[VMEM] * 3,
        scratch_shapes=[pltpu.VMEM((C, KV), BF16), pltpu.SemaphoreType.DMA((16,))],
        compiler_params=params(20),
        cost_estimate=pl.CostEstimate(flops=2_000_000_000, bytes_accessed=3_500_000, transcendentals=0),
    )(at, *parts, gain, *arrays)


def query_kernel(at_ref, normed_ref, *refs):
    arrays, (out_ref, w_ref, sems) = refs[:2], refs[2:]
    wait_copies(place(at_ref, arrays, pl.ds(0, QW), w_ref, sems))
    queries = jnp.dot(normed_ref[...], w_ref[...], preferred_element_type=F32).astype(BF16)
    for head in range(HEADS):
        out_ref[head] = queries[:, head * HEAD_SIZE : (head + 1) * HEAD_SIZE]


def project_queries(at, normed, arrays):
    return pl.pallas_call(
        query_kernel,
        out_shape=jax.ShapeDtypeStruct((HEADS, TOKENS, HEAD_SIZE), BF16),
        in_specs=[SMEM, VMEM] + [ANY] * 2,
        out_specs=VMEM,
        scratch_shapes=[pltpu.VMEM((C, QW), BF16), pltpu.SemaphoreType.DMA((16,))],
        compiler_params=params(20),
        cost_estimate=pl.CostEstimate(flops=2_000_000_000, bytes_accessed=4_500_000, transcendentals=0),
    )(at, normed, *arrays)


def attend_head(head, scale_ref, q_ref, kvs, old_refs):
    scale = scale_ref[head]
    q = q_ref[head]
    lanes = (TOKENS, HEAD_SIZE)
    scores = [
        lax.dot_general(
            q, kv[:, :HEAD_SIZE], (((1,), (1,)), ((), ())), preferred_element_type=F32
        )
        for kv in kvs
    ]
    pieces = [
        [s[:, i : i + HEAD_SIZE] for i in range(0, s.shape[1], HEAD_SIZE)] for s in scores
    ]
    best = functools.reduce(jnp.maximum, [piece for group in pieces for piece in group])
    top = jnp.broadcast_to(jnp.max(best, axis=1, keepdims=True), lanes)
    if old_refs:
        old = old_refs[0][head]
        top = jnp.maximum(top, old)
        fade = jnp.exp2((old - top) * scale)
    total = jnp.zeros(lanes, F32)
    summed = jnp.zeros(lanes, F32)
    for group, kv in zip(pieces, kvs):
        weights = []
        for piece in group:
            e = jnp.exp2((piece - top) * scale)
            total = total + e
            weights.append(e.astype(BF16))
        summed = summed + jnp.dot(
            jnp.concatenate(weights, axis=1), kv[:, HEAD_SIZE:], preferred_element_type=F32
        )
    if old_refs:
        total = total + old_refs[1][head] * fade
        summed = summed + old_refs[2][head] * fade
    return top, total, summed


def attend_all(scale_ref, q_ref, kvs, old, new):
    @pl.loop(0, HEADS, step=8)
    def _(first):
        for i in range(8):
            for ref, value in zip(new, attend_head(first + i, scale_ref, q_ref, kvs, old)):
                ref[first + i] = value


def attend_kernel(n_blocks, scale_ref, q_ref, *refs):
    attend_all(scale_ref, q_ref, refs[:n_blocks], refs[n_blocks:-3], refs[-3:])


def attend(scale, queries, kvs, state):
    return pl.pallas_call(
        functools.partial(attend_kernel, len(kvs)),
        out_shape=[jax.ShapeDtypeStruct((HEADS, TOKENS, HEAD_SIZE), F32)] * 3,
        in_specs=[SMEM] + [VMEM] * (1 + len(kvs) + len(state)),
        out_specs=[VMEM] * 3,
        compiler_params=params(16),
        cost_estimate=pl.CostEstimate(flops=6_000_000_000, bytes_accessed=6_000_000, transcendentals=2_000_000),
    )(scale, queries, *kvs, *state)


def place_kernel(n_blocks, at_ref, scale_ref, q_ref, *refs):
    arrays, kvs, refs = refs[:2], refs[2 : 2 + n_blocks], refs[2 + n_blocks :]
    old, new, w_ref, sems = refs[:3], refs[3:6], refs[6], refs[7]
    copies = place_out(at_ref, arrays, w_ref, sems)
    attend_all(scale_ref, q_ref, kvs, old, new)
    wait_copies(copies)


def attend_and_place(at, scale, queries, kvs, state, arrays):
    return pl.pallas_call(
        functools.partial(place_kernel, len(kvs)),
        out_shape=[jax.ShapeDtypeStruct((HEADS, TOKENS, HEAD_SIZE), F32)] * 3
        + [jax.ShapeDtypeStruct((QW, C), BF16)],
        in_specs=[SMEM, SMEM, VMEM, ANY, ANY] + [VMEM] * (len(kvs) + 3),
        out_specs=[VMEM] * 4,
        scratch_shapes=[pltpu.SemaphoreType.DMA((48,))],
        compiler_params=params(16),
        cost_estimate=pl.CostEstimate(flops=6_000_000_000, bytes_accessed=9_000_000, transcendentals=2_000_000),
    )(at, scale, queries, *arrays, *kvs, *state)


def finish_kernel(scale_ref, q_ref, tokens_ref, w_ref, *refs):
    kvs, old, (out_ref, context_ref) = refs[:2], refs[2:5], refs[5:]

    @pl.loop(0, HEADS, step=8)
    def _(first):
        for i in range(8):
            _, total, summed = attend_head(first + i, scale_ref, q_ref, kvs, old)
            context = summed / jnp.sum(total, axis=1, keepdims=True)
            column = pl.multiple_of((first + i) * HEAD_SIZE, HEAD_SIZE)
            context_ref[:, pl.ds(column, HEAD_SIZE)] = context.astype(BF16)

    update = jnp.dot(context_ref[...], w_ref[...], preferred_element_type=F32)
    out_ref[...] = (update + tokens_ref[...].astype(F32)).astype(BF16)


def finish(scale, queries, tokens, weights, kvs, state):
    return pl.pallas_call(
        finish_kernel,
        out_shape=jax.ShapeDtypeStruct((TOKENS, C), BF16),
        in_specs=[SMEM] + [VMEM] * (3 + len(kvs) + 3),
        out_specs=VMEM,
        scratch_shapes=[pltpu.VMEM((TOKENS, QW), BF16)],
        compiler_params=params(16),
        cost_estimate=pl.CostEstimate(flops=8_000_000_000, bytes_accessed=9_000_000, transcendentals=1_000_000),
    )(scale, queries, tokens, weights, *kvs, *state)


def on_device(
    dna_features, conv_weight, conv_bias, norm_gain, query_weight, kv_weight, out_weight, head_scale
):
    dp, seq = lax.axis_index("dp"), lax.axis_index("seq")
    core, z = dp % 2, seq % 8
    quarter = z % 2 * 2 + core
    at = jnp.stack([dp, quarter]).astype(jnp.int32)

    got = receive(conv_weight, from_core)
    start, shape = (0, 0, quarter * QUARTER), (KW, ROWS, QUARTER)
    keep, got = (lax.dynamic_slice(w, start, shape) for w in (conv_weight, got))
    unit = jnp.concatenate(
        [jnp.where(core == 0, keep, got), jnp.where(core == 0, got, keep)], axis=1
    )
    x1, x3, x2 = (receive(unit, from_x(step)) for step in (1, 3, 2))
    low, high = jnp.concatenate([unit, x1], axis=1), jnp.concatenate([x3, x2], axis=1)
    low_y = receive(low, from_y(1))
    units = low, high, low_y, receive(high, from_y(-1))

    even = z % 2 == 0
    rows = dna_features.reshape(TOKENS, 2 * CIN)
    rows_z = receive(rows, from_z_pair)
    edge = pack([jnp.where(even, rows[:1], rows[-1:])], [x1])
    beside = [p for i in range(1, 15, 2) for p in ((i, i + 1), (i + 1, i))]
    beyond = [(i, i - 2) for i in range(2, 16, 2)] + [(i, i + 2) for i in range(1, 14, 2)]
    beside, beyond = (lax.ppermute(edge, "seq", pairs) for pairs in (beside, beyond))

    def between(block, before, behind):
        return jnp.concatenate([before, block, behind], axis=0)

    pair_rows = between(
        rows_z, jnp.where(even, rows[-1:], beyond), jnp.where(even, beyond, rows[:1])
    )
    own_rows = between(
        rows, jnp.where(even, beside, rows_z[-1:]), jnp.where(even, rows_z[:1], beside)
    )
    far, near = (
        jnp.stack([jnp.concatenate([r[:TOKENS], r[1 : TOKENS + 1], r[2:]], axis=1) for r in pair])
        for pair in ((receive(pair_rows, from_core), pair_rows), (receive(own_rows, from_core), own_rows))
    )
    bias = lax.dynamic_slice(conv_bias.reshape(1, C), (0, quarter * QUARTER), (1, QUARTER))

    packed = pack_weights(query_weight, kv_weight, out_weight, high)
    px1, px3 = receive(packed, from_x(1)), receive(packed, from_x(3))
    low = jnp.concatenate([packed, px1], axis=0)
    low_y = receive(low, from_y(1))
    px2 = receive(px3, from_x(1))
    py3, py2 = (receive(rows[:, : QW + KV], from_y(-1)) for rows in (px3, px2))
    projections = low, px3, px2, low_y, py3, py2
    high_out = jnp.concatenate([px3[:, QW + KV :], px2[:, QW + KV :]], axis=0)
    out_rows = low, high_out, low_y, receive(high_out, from_y(-1))

    t_d, t_z, whole = convolve_first(at[:1] // 2, far, bias, units)
    got_z, got_d = receive(t_z, from_z_pair), receive(t_d, from_diagonal)
    t_c, t_own = convolve(near, bias, whole)
    projections = stack(projections, QW + KV, [t_c, got_z, got_d])
    projections = projections, receive(projections, from_core)
    parts = t_own, receive(t_c, from_core), got_z, got_d
    tokens, normed, pairs = norm_and_pairs(at, parts, norm_gain.reshape(1, C), projections)

    queries = project_queries(at, normed, projections)
    scale = head_scale * (LOG2E / math.sqrt(HEAD_SIZE))

    both = stack([pairs, receive(pairs, from_y_hi)], KV, [queries])
    below, above = receive(both, from_z(-1)), receive(both, from_z(1))
    out_rows = stack(out_rows, QW, [below, above], last=True)
    out_rows = out_rows, receive(out_rows, from_core)
    state = attend(scale, queries, [both, below, above], ())
    below, above = receive(below, from_z(-1)), receive(above, from_z(1))
    state = attend(scale, queries, [below, above], state)
    below, above = receive(below, from_z(-1)), receive(above, from_z(1))
    last = [receive(below[:TOKENS], from_z(-1)), receive(above[TOKENS:], from_z(1))]
    *state, out_weights = attend_and_place(at, scale, queries, [below, above], state, out_rows)
    encoded = finish(scale, queries, tokens, out_weights, last, state)
    return tokens[None], encoded[None]


def solution(mesh):
    in_specs = (
        P("dp", "seq", None),
        P(None, "dp", None),
        P(),
        P(),
        P("dp", None),
        P("dp", None),
        P("dp", None),
        P(),
    )
    out_specs = (P("dp", "seq", None), P("dp", "seq", None))
    return jax.shard_map(
        on_device, mesh=mesh, in_specs=in_specs, out_specs=out_specs, check_vma=False
    )
```
